256 devices in a mesh: ctx: 8 (over y, core), exp: 32 (over z, x).
Axes of the slice: x: 4, y: 4, z: 8, core: 2. Of those that a mesh axis runs over, the one named last changes fastest.
Arguments:
- tokens: bfloat16 [32, 1024, 2560], P('exp', 'ctx'), may hold values from -6 to 6
- router: bfloat16 [2560, 64], replicated, may hold values from -0.125 to 0.125
- expert_gate_up: bfloat16 [64, 2560, 512], P('exp', 'ctx'), may hold values from -0.125 to 0.125
- expert_down: bfloat16 [64, 256, 2560], P('exp', 'ctx'), may hold values from -0.375 to 0.375
- shared_gate_up: bfloat16 [2560, 512], replicated, may hold values from -0.125 to 0.125
- shared_down: bfloat16 [256, 2560], replicated, may hold values from -0.375 to 0.375
- expert_index_table: int32 [32, 1024, 8], P('exp', 'ctx'), may hold values from 0 to 63, all different within a row; in each aligned block of 128 rows (0 to 127, 128 to 255, ..., all dimensions but the last counted through in order) at most 20 rows name the same one
- document_length_table: int32 [32, 8], P('exp'), may hold values from 1 to 512, 1024 in all within a row
- step_sizes_unsoftened: float32 [32, 1024, 40], P('exp', 'ctx'), may hold values from -4 to 4
- state_input_vectors: bfloat16 [32, 1024, 128], P('exp', 'ctx'), may hold values from -0.8984375 to 0.8984375
- state_output_vectors: bfloat16 [32, 1024, 128], P('exp', 'ctx'), may hold values from -0.5 to 0.5
- decay_rate: float32 [40], replicated, may hold values from 0.00048828125 to 0.05
- skip_gain: float32 [40], replicated, may hold values from 0.25 to 1
- cotangent: bfloat16 [32, 1024, 2560], P('exp', 'ctx'), may hold values from -6 to 6
Outputs:
- mixed: bfloat16 [32, 1024, 2560], P('exp', 'ctx')
- input_grad: bfloat16 [32, 1024, 2560], P('exp', 'ctx')
The draws below stay inside these ranges and needn't reach their ends.
Inputs may be any that keep to these rules, and one draw needn't show every extreme that they name: `expert_index_table`: in each aligned block of 128 positions (those of one device) each position names 8 different experts and no expert is named more than 20 times; some expert is named exactly 20 times. `document_length_table`: each row's lengths sum to 1024.
All inputs are finite; a program needn't handle non-finite values.
Results may differ from the reference program's by a relative error of at most 0.008.
Values may be sent and summed in bfloat16 or wider, within the bound.
A program may use at most 128 MiB of HBM per device.

```python
import math
import jax
import jax.numpy as jnp
import numpy as np
from jax import lax

MIXER_HEADS = 40
HEAD_STATE_SIZE = 128
TOKEN_FEATURES = 2560
F = 256
FS = 256
ROUTED_EXPERTS = 64
CHOSEN_EXPERTS = 8
DEVICE_TOKENS = 128
ROW_DOCUMENTS = 8
PACKED_LENGTH = 1024
PACKED_ROWS = 32
LONGEST_DOCUMENT = 512
EXPERT_SLOTS = 20


def block_scale(own_key, dims, cuts, low, top_value):
    gain = 1.0
    for position, parts in cuts:
        steps = jax.random.uniform(jax.random.fold_in(jax.random.fold_in(own_key, 6), position), (parts,), jnp.float32, low / len(cuts), top_value / len(cuts))
        gain = gain * jnp.repeat(jnp.exp(steps), dims[position] // parts).reshape((-1,) + (1,) * (len(dims) - 1 - position))
    return gain


def length_profile(count, total, reach, skew):
    weights = [(1 << 20) // math.isqrt(standing ** skew) + 1 for standing in range(2, count + 1)]
    surplus, given = total - reach - (count - 1), [1] * (count - 1)
    while surplus > 0:
        free = [i for i in range(count - 1) if given[i] < reach]
        pool, left = sum([weights[i] for i in free]), surplus
        for i in free:
            more = min(reach - given[i], max(1, left * weights[i] // pool), surplus)
            given[i] = given[i] + more
            surplus = surplus - more
    return np.array([reach] + given)


def ragged_sizes(stream_key, count, total, reach, slope):
    if count == 2:
        one = jax.random.randint(stream_key, (), max(1, total - reach), min(reach, total - 1) + 1)
        return jnp.stack([one, total - one])
    sizes = jnp.asarray(length_profile(count, total, reach, slope), jnp.int32)
    twos = (count - 1) // 2
    giver, taker = sizes[1:1 + 2 * twos:2], sizes[2:2 + 2 * twos:2]
    room = jnp.minimum(giver - 1, reach - taker)
    moved = jax.random.randint(jax.random.fold_in(stream_key, 1), (twos,), 0, 1 << 20) % (room + 1)
    sizes = sizes.at[1:1 + 2 * twos:2].set(giver - moved).at[2:2 + 2 * twos:2].set(taker + moved)
    return sizes[jax.random.permutation(jax.random.fold_in(stream_key, 2), count)]


def deal_out(key, own, number, rows, number_of, top, most, skew):
    ranking = jax.random.permutation(key, number_of)
    heavy_load, usual = portions_of(number_of, rows * top, most, skew, True), portions_of(number_of, rows * top, most, skew, False)
    places = jnp.arange(number_of)

    def named(sizes, offset_by):
        used = int((sizes > 0).sum())
        fixed = max(1, used // 4)
        passed = fixed + (places - fixed + offset_by * (used - fixed)) % max(1, number_of - fixed)
        return jnp.zeros((number_of,), jnp.int32).at[ranking[jnp.where(places < fixed, places, passed)]].set(jnp.asarray(sizes, jnp.int32))

    sizes = jnp.where(number % 4 == 0, named(heavy_load, number // 4), named(usual, number - number // 4 - 1))
    mixed = jax.random.permutation(jax.random.fold_in(own, 3), number_of)
    donor, taker = mixed[0:number_of // 2 * 2:2], mixed[1:number_of // 2 * 2:2]
    room = jnp.minimum(sizes[donor] - 1, most - sizes[taker]) // 2
    room = jnp.where((donor == ranking[0]) | (taker == ranking[0]) | (sizes[taker] == 0), 0, jnp.maximum(room, 0))
    passed = jax.random.randint(jax.random.fold_in(own, 4), (number_of // 2,), 0, 1 << 20) % (room + 1)
    sizes = sizes.at[donor].add(-passed).at[taker].add(passed)
    labels = jnp.searchsorted(jnp.cumsum(sizes), jnp.arange(rows * top), side="right").astype(jnp.int32)
    grid = labels.reshape(top, rows).T
    grid = grid[jax.random.permutation(jax.random.fold_in(own, 1), rows)]
    offset_by = jax.random.randint(jax.random.fold_in(own, 2), (rows, 1), 0, top)
    return jnp.take_along_axis(grid, (jnp.arange(top)[None, :] + offset_by) % top, axis=1)


def portions_of(number_of, total, limit, skew, full):
    portions = [(1 << 20) // math.isqrt(grade ** skew) + 1 for grade in range(1, number_of + 1)]
    largest = limit if full else min(limit, max(-(-total // number_of), total * portions[0] // sum(portions)))
    least = 1 if total - largest >= number_of - 1 else 0
    holding, spare = [largest] + [least] * (number_of - 1), total - largest - least * (number_of - 1)
    while spare > 0:
        candidates = [i for i in range(1, number_of) if holding[i] < largest] or [i for i in range(1, number_of) if holding[i] < limit]
        whole, remaining = sum([portions[i] for i in candidates]), spare
        for i in candidates:
            extra = min(limit - holding[i], max(1, remaining * portions[i] // whole), spare)
            holding[i] = holding[i] + extra
            spare = spare - extra
    return np.array(holding)


def scatter_about(rng, shape, deviation, bound, cuts=(), kind=jnp.bfloat16):
    factor_of = block_scale(rng, shape, cuts, -0.22, 0.18) if cuts else 1.0
    entries = jax.random.normal(rng, shape, jnp.float32) * deviation * factor_of
    return jnp.minimum(jnp.maximum(entries, -bound), bound).astype(kind)


def setup_inputs(seed: int = 0) -> dict:
    key_of = jax.random.split(jax.random.key(seed), 15)
    tokens = scatter_about(key_of[0], (PACKED_ROWS, PACKED_LENGTH, TOKEN_FEATURES), 1.0, 6.0, ((0, 32), (1, 8)))
    router = scatter_about(key_of[1], (TOKEN_FEATURES, ROUTED_EXPERTS), TOKEN_FEATURES ** -0.5, 0.125)
    expert_gate_up = scatter_about(key_of[2], (ROUTED_EXPERTS, TOKEN_FEATURES, 2 * F), TOKEN_FEATURES ** -0.5, 0.125, ((0, 32), (1, 8)))
    expert_down = scatter_about(key_of[3], (ROUTED_EXPERTS, F, TOKEN_FEATURES), F ** -0.5, 0.375, ((0, 32), (1, 8)))
    shared_gate_up = scatter_about(key_of[4], (TOKEN_FEATURES, 2 * FS), TOKEN_FEATURES ** -0.5, 0.125)
    shared_down = scatter_about(key_of[5], (FS, TOKEN_FEATURES), FS ** -0.5, 0.375)
    expert_index_table_keys = jax.random.split(jax.random.fold_in(key_of[6], 1), PACKED_ROWS * PACKED_LENGTH // DEVICE_TOKENS)
    expert_index_table_turns = jax.random.permutation(jax.random.fold_in(key_of[6], 3), PACKED_ROWS * PACKED_LENGTH // DEVICE_TOKENS)
    expert_index_table = jax.vmap(lambda own, number: deal_out(jax.random.fold_in(key_of[6], 2), own, number, DEVICE_TOKENS, ROUTED_EXPERTS, CHOSEN_EXPERTS, EXPERT_SLOTS, 1))(expert_index_table_keys, expert_index_table_turns).reshape((PACKED_ROWS, PACKED_LENGTH, CHOSEN_EXPERTS))
    document_length_table = jax.vmap(lambda own: ragged_sizes(own, ROW_DOCUMENTS, PACKED_LENGTH, LONGEST_DOCUMENT, 2))(jax.random.split(key_of[7], PACKED_ROWS)).reshape((PACKED_ROWS, ROW_DOCUMENTS)).astype(jnp.int32)
    step_sizes_unsoftened = scatter_about(key_of[8], (PACKED_ROWS, PACKED_LENGTH, MIXER_HEADS), 1.0, 4.0, ((0, 32), (1, 8)), jnp.float32)
    state_input_vectors = scatter_about(key_of[9], (PACKED_ROWS, PACKED_LENGTH, HEAD_STATE_SIZE), 0.15, 0.8984375, ((0, 32), (1, 8)))
    state_output_vectors = scatter_about(key_of[10], (PACKED_ROWS, PACKED_LENGTH, HEAD_STATE_SIZE), HEAD_STATE_SIZE ** -0.5, 0.5, ((0, 32), (1, 8)))
    decay_rate = jnp.clip(jnp.exp(jax.random.uniform(key_of[11], (MIXER_HEADS,), jnp.float32, math.log(0.00048828125), math.log(0.05))), 0.00048828125, 0.05)
    skip_gain = jnp.clip(jax.random.uniform(key_of[12], (MIXER_HEADS,), jnp.float32, 0.25, 1.0), 0.25, 1.0)
    cotangent = scatter_about(key_of[13], (PACKED_ROWS, PACKED_LENGTH, TOKEN_FEATURES), 1.0, 6.0, ((0, 32), (1, 8)))
    return dict(tokens=tokens, router=router, expert_gate_up=expert_gate_up, expert_down=expert_down, shared_gate_up=shared_gate_up, shared_down=shared_down, expert_index_table=expert_index_table, document_length_table=document_length_table, step_sizes_unsoftened=step_sizes_unsoftened, state_input_vectors=state_input_vectors, state_output_vectors=state_output_vectors, decay_rate=decay_rate, skip_gain=skip_gain, cotangent=cotangent)


highest = lax.Precision.HIGHEST

def expert_hidden(rows, gate_up, units):
    product = jnp.dot(rows, gate_up, preferred_element_type=jnp.float32)
    return (jax.nn.silu(product[:, :units]) * product[:, units:]).astype(jnp.bfloat16)

def document_index(starts, positions):
    return lax.optimization_barrier(jnp.sum((starts[None, :] <= positions[:, None]).astype(jnp.int32), axis=1)) - 1

def state_block(carry_state, block_inputs, decay_rate):
    values, step_sizes, writes, read_vectors, documents, before = block_inputs
    cumulative = jnp.cumsum(-step_sizes * decay_rate[None, :], axis=0)
    token_order = jnp.arange(documents.shape[0], dtype=jnp.int32)
    causal = (documents[:, None] == documents[None, :]) & (token_order[:, None] >= token_order[None, :])
    spread = cumulative.T[:, :, None] - cumulative.T[:, None, :]
    decayed = jnp.where(causal[None], jnp.exp(jnp.where(causal[None], spread, 0.0)), 0.0)
    affinity = jnp.einsum('tn,sn->ts', read_vectors, writes, precision=highest)
    weights = affinity[None] * decayed * step_sizes.T[:, None, :]
    output = jnp.einsum('hts,shp->thp', weights, values, precision=highest)
    carried = jnp.exp(cumulative) * (documents == before).astype(jnp.float32)[:, None]
    output = output + carried[:, :, None] * jnp.einsum('hpn,tn->thp', carry_state, read_vectors, precision=highest)
    closing = jnp.exp(cumulative[-1][None, :] - cumulative) * (documents == documents[-1]).astype(jnp.float32)[:, None] * step_sizes
    keep_factor = jnp.exp(cumulative[-1]) * (documents[-1] == before).astype(jnp.float32)
    carry_state = keep_factor[:, None, None] * carry_state + jnp.einsum('sh,shp,sn->hpn', closing, values, writes, precision=highest)
    return (carry_state, output)

def mixer_row(values_row, raw_steps, writes, read_vectors, lengths, decay_rate, skip_gain):
    row_length = values_row.shape[0]
    head_count = decay_rate.shape[0]
    step_sizes = jax.nn.softplus(raw_steps)
    starts = jnp.cumsum(lengths) - lengths
    positions = jnp.arange(row_length, dtype=jnp.int32)
    documents = document_index(starts, positions)
    before = document_index(starts, positions - 1)
    block_rows = min(128, DEVICE_TOKENS)
    block_count = row_length // block_rows
    shaped = values_row.reshape(row_length, head_count, -1)
    inputs = (shaped.reshape(block_count, block_rows, head_count, -1), step_sizes.reshape(block_count, block_rows, head_count), writes.reshape(block_count, block_rows, -1), read_vectors.reshape(block_count, block_rows, -1), documents.reshape(block_count, block_rows), before.reshape(block_count, block_rows)[:, 0])

    def advance(carry_state, block_inputs):
        return state_block(carry_state, block_inputs, decay_rate)
    initial = jnp.zeros((head_count, shaped.shape[2], writes.shape[1]), jnp.float32)
    final_state, outputs = lax.scan(advance, initial, inputs)
    outputs = outputs.reshape(row_length, head_count, -1) + skip_gain[None, :, None] * shaped
    return outputs.reshape(row_length, -1)

def reference(tokens, router, expert_gate_up, expert_down, shared_gate_up, shared_down, expert_index_table, document_length_table, step_sizes_unsoftened, state_input_vectors, state_output_vectors, decay_rate, skip_gain, cotangent):
    flattened_token_rows = tokens.reshape(-1, TOKEN_FEATURES)
    token_total = flattened_token_rows.shape[0]
    logits = jnp.dot(flattened_token_rows, router, preferred_element_type=jnp.float32)
    routes = expert_index_table.reshape(-1, CHOSEN_EXPERTS)
    chosen = routes[:, :, None] == jnp.arange(ROUTED_EXPERTS, dtype=jnp.int32)[None, None, :]
    picked = lax.optimization_barrier(jnp.sum(jnp.where(chosen, logits[:, None, :], 0.0), axis=2))
    sigmoids = jax.nn.sigmoid(picked)
    gate_values = sigmoids / lax.optimization_barrier(jnp.sum(sigmoids, axis=1, keepdims=True))
    block_total = token_total // DEVICE_TOKENS
    flag_table = chosen.reshape(block_total, DEVICE_TOKENS * CHOSEN_EXPERTS, ROUTED_EXPERTS).astype(jnp.int32)
    slot_index = lax.optimization_barrier(jnp.sum(flag_table * (jnp.cumsum(flag_table, axis=1) - 1), axis=2))
    destination = (jnp.arange(block_total, dtype=jnp.int32)[:, None] * EXPERT_SLOTS + slot_index).reshape(-1)
    owners = jnp.repeat(jnp.arange(token_total, dtype=jnp.int32), CHOSEN_EXPERTS)
    flat_routes = routes.reshape(-1)
    row_table = jnp.full((ROUTED_EXPERTS, block_total * EXPERT_SLOTS), -1, jnp.int32).at[flat_routes, destination].set(owners)
    gate_table = jnp.zeros((ROUTED_EXPERTS, block_total * EXPERT_SLOTS), jnp.float32).at[flat_routes, destination].set(gate_values.reshape(-1))

    def route_expert(accumulated, expert_inputs):
        rows, scales, gate_up, down = expert_inputs
        valid = rows >= 0
        safe_rows = jnp.maximum(rows, 0)
        gathered = jnp.where(valid[:, None], flattened_token_rows[safe_rows], jnp.zeros((), jnp.bfloat16))
        hidden = expert_hidden(gathered, gate_up, F)
        produced = jnp.dot(hidden, down, preferred_element_type=jnp.float32).astype(jnp.bfloat16)
        return (accumulated.at[safe_rows].add(scales[:, None] * produced.astype(jnp.float32)), None)
    routed_output, unused = lax.scan(route_expert, jnp.zeros((token_total, TOKEN_FEATURES), jnp.float32), (row_table, gate_table, expert_gate_up, expert_down))
    shared_expert_output = jnp.dot(expert_hidden(flattened_token_rows, shared_gate_up, FS), shared_down, preferred_element_type=jnp.float32)
    mixer_input_rows = (flattened_token_rows.astype(jnp.float32) + shared_expert_output + routed_output).astype(jnp.bfloat16).reshape(PACKED_ROWS, PACKED_LENGTH, TOKEN_FEATURES)

    def forward(values):
        return jax.vmap(mixer_row, in_axes=(0, 0, 0, 0, 0, None, None))(values, step_sizes_unsoftened, state_input_vectors.astype(jnp.float32), state_output_vectors.astype(jnp.float32), document_length_table, decay_rate, skip_gain)
    outputs, pullback = jax.vjp(forward, mixer_input_rows.astype(jnp.float32))
    gradient = pullback(cotangent.astype(jnp.float32))[0]
    return (outputs.astype(jnp.bfloat16), gradient.astype(jnp.bfloat16))
```

```python
import functools

import jax
import jax.numpy as jnp
from jax import lax
from jax.experimental import pallas as pl
from jax.experimental.pallas import tpu as pltpu
from jax.sharding import PartitionSpec as P

highest = lax.Precision.HIGHEST
MESH = pl.DeviceIdType.MESH
F32 = jnp.float32
BF16 = jnp.bfloat16

T = 128
D = 2560
E = 64
K = 8
FH = 256
NZ, NX, NY = 8, 4, 4
GR = D // 8
DR = FH // 8
H = D // 2
SLOT = {4: 0, 3: 1, -3: 2, 2: 3, -2: 4, 1: 5, -1: 6, 0: 7}


def expert_kernel(
    x_hbm, router_ref, gu_hbm, dn_hbm, sgu_ref, sdn_ref, idx_ref, out_ref,
    xall, gall, wg, wd, hid, part, shared, rr, rl, sr, sl_, loc, ss, rs,
):
    ctx = lax.axis_index("ctx")
    exp = lax.axis_index("exp")
    z, x = exp // NX, exp % NX
    y, core = ctx // 2, ctx % 2
    zp = {"exp": (exp + NX) % (NX * NZ)}
    zm = {"exp": (exp + NX * (NZ - 1)) % (NX * NZ)}
    xp = {"exp": z * NX + (x + 1) % NX}
    xm = {"exp": z * NX + (x + NX - 1) % NX}
    yp = {"ctx": (ctx + 2) % 8}
    ym = {"ctx": (ctx + 6) % 8}
    sib = {"ctx": ctx + 1 - 2 * core}
    y1, y2, y3 = (y + 1) % NY, (y + 2) % NY, (y + 3) % NY
    other = 1 - core

    counter = [0]

    def rcopy(src, dst, dev, k):
        return pltpu.make_async_remote_copy(
            src_ref=src, dst_ref=dst, send_sem=ss.at[k], recv_sem=rs.at[k],
            device_id=dev, device_id_type=MESH,
        )

    sent = []

    def send(src, dst, dev):
        k = counter[0]
        counter[0] += 1
        c = rcopy(src, dst, dev, k)
        c.start()
        sent.append(c)
        return k

    def arrived(k, region):
        rcopy(region, region, sib, k).wait_recv()

    barrier = pltpu.get_barrier_semaphore()
    for dev in (zp, zm, xp, xm, yp, ym, sib):
        pl.semaphore_signal(barrier, inc=1, device_id=dev, device_id_type=MESH)
    pl.semaphore_wait(barrier, 7)

    x_own = xall.at[SLOT[0]]
    lx = pltpu.make_async_copy(x_hbm.at[0], x_own, loc.at[0])
    lx.start()
    kx = {}
    kx[-1] = send(x_hbm.at[0], xall.at[SLOT[-1]], zp)
    kx[1] = send(x_hbm.at[0], xall.at[SLOT[1]], zm)
    own = {}
    for name, hbm, w in (("g", gu_hbm, wg), ("d", dn_hbm, wd)):
        own[name, "A", 2] = send(hbm.at[0], w.at[2, 0, y, core], xp)
        own[name, "A", 1] = send(hbm.at[0], w.at[1, 0, y, core], xm)
        own[name, "B", 3] = send(hbm.at[1], w.at[0, 1, y, core], yp)
        own[name, "B", 1] = send(hbm.at[1], w.at[0, 1, y, core], ym)
        own[name, "S"] = send(hbm, w.at[0, :, y, core], sib)
    lg = pltpu.make_async_copy(gu_hbm, wg.at[0, :, y, core], loc.at[1])
    ld = pltpu.make_async_copy(dn_hbm, wd.at[0, :, y, core], loc.at[2])
    lg.start()
    ld.start()

    lx.wait()
    xo = x_own[...]
    logits = jnp.dot(xo, router_ref[...], preferred_element_type=F32)
    lane = lax.broadcasted_iota(jnp.int32, (T, E), 1)
    chosen = jnp.zeros((T, E), F32)
    idx = idx_ref[0]
    for j in range(K):
        chosen = chosen + jnp.where(idx[:, j : j + 1] == lane, 1.0, 0.0)
    sig = chosen * jax.nn.sigmoid(logits)
    gate = sig / jnp.sum(sig, axis=1, keepdims=True)
    hi = gate.astype(BF16)
    lo = (gate - hi.astype(F32)).astype(BF16)
    gall[SLOT[0], :, 0:E] = hi
    gall[SLOT[0], :, E : 2 * E] = lo
    kg = {}
    kg[-1] = send(gall.at[SLOT[0]], gall.at[SLOT[-1]], zp)
    kg[1] = send(gall.at[SLOT[0]], gall.at[SLOT[1]], zm)

    sp = jnp.dot(xo, sgu_ref[...], preferred_element_type=F32)
    sh = (jax.nn.silu(sp[:, :FH]) * sp[:, FH:]).astype(BF16)
    shared[...] = xo.astype(F32) + jnp.dot(sh, sdn_ref[...], preferred_element_type=F32)

    half = {}
    row = {"g": (wg, GR), "d": (wd, DR)}

    def first_ring(name):
        w, n = row[name]
        h = n // 2
        lo_, hi_ = pl.ds(0, h), pl.ds(h, h)
        arrived(own[name, "A", 2], w.at[2, 0, y, core])
        half[name, "A", 2] = send(w.at[2, 0, y, core, lo_], w.at[3, 0, y, core, lo_], xp)
        arrived(own[name, "A", 1], w.at[1, 0, y, core])
        half[name, "A", 1] = send(w.at[1, 0, y, core, hi_], w.at[3, 0, y, core, hi_], xm)
        arrived(own[name, "B", 3], w.at[0, 1, y3, core])
        half[name, "B", 3] = send(w.at[0, 1, y3, core, lo_], w.at[0, 1, y3, core, lo_], yp)
        arrived(own[name, "B", 1], w.at[0, 1, y1, core])
        half[name, "B", 1] = send(w.at[0, 1, y1, core, hi_], w.at[0, 1, y1, core, hi_], ym)
        own[name, "B", 3, "S"] = send(w.at[0, 1, y3, core], w.at[0, 1, y3, core], sib)
        own[name, "B", 1, "S"] = send(w.at[0, 1, y1, core], w.at[0, 1, y1, core], sib)

    slab = {}

    def second_ring(name):
        w, n = row[name]
        h = n // 2
        lo_, hi_ = pl.ds(0, h), pl.ds(h, h)
        arrived(half[name, "A", 2], w.at[3, 0, y, core, lo_])
        arrived(half[name, "A", 1], w.at[3, 0, y, core, hi_])
        a = w.at[:, 0, y, core]
        slab[name, "A", 3] = send(a, a, yp)
        slab[name, "A", 1] = send(a, a, ym)
        arrived(half[name, "B", 3], w.at[0, 1, y2, core, lo_])
        arrived(half[name, "B", 1], w.at[0, 1, y2, core, hi_])
        b = w.at[0, 1, :, core]
        slab[name, "B", 2] = send(b, w.at[2, 1, :, core], xp)
        slab[name, "B", 1] = send(b, w.at[1, 1, :, core], xm)
        s = w.at[pl.ds(1, 3), 0, y, core]
        slab[name, "A", 0, "S"] = send(s, s, sib)
        s = w.at[0, 1, y2, core]
        slab[name, "B", 0, "S"] = send(s, s, sib)

    last = {}

    def third(name):
        w, n = row[name]
        a3, a1 = w.at[:, 0, y3, core], w.at[:, 0, y1, core]
        arrived(slab[name, "A", 3], a3)
        s = w.at[pl.ds(0, 2), 0, y3, core]
        last[name, "A", 3] = send(s, s, yp)
        arrived(slab[name, "A", 1], a1)
        s = w.at[pl.ds(2, 2), 0, y1, core]
        last[name, "A", 1] = send(s, s, ym)
        b2, b1 = w.at[2, 1, :, core], w.at[1, 1, :, core]
        arrived(slab[name, "B", 2], b2)
        last[name, "B", 2] = send(w.at[2, 1, pl.ds(0, 2), core], w.at[3, 1, pl.ds(0, 2), core], xp)
        arrived(slab[name, "B", 1], b1)
        last[name, "B", 1] = send(w.at[1, 1, pl.ds(2, 2), core], w.at[3, 1, pl.ds(2, 2), core], xm)
        for key, s in (("A3", a3), ("A1", a1), ("B2", b2), ("B1", b1)):
            last[name, key, "S"] = send(s, s, sib)

    fin = {}

    def fourth(name):
        w, n = row[name]
        arrived(last[name, "A", 3], w.at[pl.ds(0, 2), 0, y2, core])
        arrived(last[name, "A", 1], w.at[pl.ds(2, 2), 0, y2, core])
        s = w.at[:, 0, y2, core]
        fin[name, "A", "S"] = send(s, s, sib)
        arrived(last[name, "B", 2], w.at[3, 1, pl.ds(0, 2), core])
        arrived(last[name, "B", 1], w.at[3, 1, pl.ds(2, 2), core])
        s = w.at[3, 1, :, core]
        fin[name, "B", "S"] = send(s, s, sib)

    def from_sibling(name):
        w, n = row[name]
        arrived(own[name, "S"], w.at[0, :, y, other])
        arrived(own[name, "B", 3, "S"], w.at[0, 1, y3, other])
        arrived(own[name, "B", 1, "S"], w.at[0, 1, y1, other])
        arrived(slab[name, "A", 0, "S"], w.at[pl.ds(1, 3), 0, y, other])
        arrived(slab[name, "B", 0, "S"], w.at[0, 1, y2, other])
        arrived(last[name, "A3", "S"], w.at[:, 0, y3, other])
        arrived(last[name, "A1", "S"], w.at[:, 0, y1, other])
        arrived(last[name, "B2", "S"], w.at[2, 1, :, other])
        arrived(last[name, "B1", "S"], w.at[1, 1, :, other])
        arrived(fin[name, "A", "S"], w.at[:, 0, y2, other])
        arrived(fin[name, "B", "S"], w.at[3, 1, :, other])

    def token_step(d):
        for buf, keys in ((xall, kx), (gall, kg)):
            arrived(keys[-d], buf.at[SLOT[-d]])
            arrived(keys[d], buf.at[SLOT[d]])
            if d < 3:
                keys[-d - 1] = send(buf.at[SLOT[-d]], buf.at[SLOT[-d - 1]], zp)
                keys[d + 1] = send(buf.at[SLOT[d]], buf.at[SLOT[d + 1]], zm)
            else:
                lo_, hi_ = pl.ds(0, T // 2), pl.ds(T // 2, T // 2)
                keys["lo"] = send(buf.at[SLOT[-3], lo_], buf.at[SLOT[4], lo_], zp)
                keys["hi"] = send(buf.at[SLOT[3], hi_], buf.at[SLOT[4], hi_], zm)

    lg.wait()
    ld.wait()
    first_ring("g")
    second_ring("g")
    token_step(1)
    first_ring("d")
    second_ring("d")
    token_step(2)
    third("g")
    token_step(3)
    for buf, keys in ((xall, kx), (gall, kg)):
        arrived(keys["lo"], buf.at[SLOT[4], pl.ds(0, T // 2)])
        arrived(keys["hi"], buf.at[SLOT[4], pl.ds(T // 2, T // 2)])
    fourth("g")
    from_sibling("g")

    MT = 256

    def hidden(n, _):
        slot, e = n // 2, n % 2
        expert = 2 * (z * NX + (x + jnp.where(slot == 2, 3, jnp.where(slot == 3, 2, slot))) % NX) + e
        r = lax.broadcasted_iota(jnp.int32, (2 * E, FH), 0)
        sel = jnp.where((r == expert) | (r == expert + E), 1.0, 0.0).astype(BF16)

        def tile(m, _):
            xs = xall[pl.ds(m * (MT // T), MT // T)].reshape(MT, D)
            gs = gall[pl.ds(m * (MT // T), MT // T)].reshape(MT, 2 * E)
            w = wg[slot, e].reshape(D, 2 * FH)
            p = jnp.dot(xs, w, preferred_element_type=F32)
            g = jnp.dot(gs, sel, preferred_element_type=F32)
            h = (jax.nn.silu(p[:, :FH]) * p[:, FH:] * g).astype(BF16)
            hid[slot, e, pl.ds(pl.multiple_of(m * MT, MT), MT), :] = h
            return 0

        lax.fori_loop(0, NZ * T // MT, tile, 0)
        return 0

    lax.fori_loop(0, 4, hidden, 0)
    third("d")
    lax.fori_loop(4, 8, hidden, 0)
    fourth("d")
    from_sibling("d")

    NC = 256

    def partial(first, rows):
        def tile(c, _):
            cols = pl.ds(pl.multiple_of(c * NC, NC), NC)
            acc = jnp.zeros((rows, NC), F32)
            for slot in range(4):
                for e in range(2):
                    acc = acc + jnp.dot(
                        hid[slot, e, pl.ds(first * T, rows), :],
                        wd[slot, e, :, :, :, cols].reshape(FH, NC),
                        preferred_element_type=F32,
                    )
            part[pl.ds(0, rows), cols] = acc
            return 0

        lax.fori_loop(0, D // NC, tile, 0)

    c0, c1 = pl.ds(0, H), pl.ds(H, H)
    kr, kl = {}, {}
    partial(SLOT[4], T)
    sr[0] = part[0:T, c0].astype(BF16)
    kr[0] = send(sr.at[0], rr.at[0], zp)
    sl_[0] = part[0:T, c1].astype(BF16)
    kl[0] = send(sl_.at[0], rl.at[0], zm)
    partial(SLOT[3], 2 * T)
    sr[1] = part[0:T, c1].astype(BF16)
    kr[1] = send(sr.at[1], rr.at[1], zp)
    sl_[1] = part[T : 2 * T, c0].astype(BF16)
    kl[1] = send(sl_.at[1], rl.at[1], zm)

    def relay(k, cr, cl):
        arrived(kr[k], rr.at[k])
        rr[k] = (rr[k].astype(F32) + part[0:T, cr]).astype(BF16)
        kr[k + 2] = send(rr.at[k], rr.at[k + 2], zp)
        arrived(kl[k], rl.at[k])
        rl[k] = (rl[k].astype(F32) + part[T : 2 * T, cl]).astype(BF16)
        kl[k + 2] = send(rl.at[k], rl.at[k + 2], zm)

    relay(0, c0, c1)
    partial(SLOT[2], 2 * T)
    relay(1, c1, c0)
    relay(2, c0, c1)
    partial(SLOT[1], 2 * T)
    relay(3, c1, c0)
    relay(4, c0, c1)
    partial(SLOT[0], T)
    for k, cr, cl in ((5, c1, c0), (6, c0, c1)):
        arrived(kr[k], rr.at[k])
        arrived(kl[k], rl.at[k])
        part[0:T, cr] += rr[k].astype(F32)
        part[0:T, cl] += rl[k].astype(F32)
    out_ref[...] = (part[0:T, :] + shared[...]).astype(BF16)
    for c in sent:
        c.wait_send()


COPIES = 2 + 10 + 2 + 2 * (6 + 6 + 8 + 2) + 12 + 14


def routed_and_shared(tokens, router, gate_up, down, shared_gate_up, shared_down, routes):
    vmem = pl.BlockSpec(memory_space=pltpu.VMEM)
    hbm = pl.BlockSpec(memory_space=pl.ANY)
    return pl.pallas_call(
        expert_kernel,
        out_shape=jax.ShapeDtypeStruct((T, D), BF16),
        in_specs=[hbm, vmem, hbm, hbm, vmem, vmem, vmem],
        out_specs=vmem,
        scratch_shapes=[
            pltpu.VMEM((NZ, T, D), BF16),
            pltpu.VMEM((NZ, T, 2 * E), BF16),
            pltpu.VMEM((NX, 2, NY, 2, GR, 2 * FH), BF16),
            pltpu.VMEM((NX, 2, NY, 2, DR, D), BF16),
            pltpu.VMEM((NX, 2, NZ * T, FH), BF16),
            pltpu.VMEM((2 * T, D), F32),
            pltpu.VMEM((T, D), F32),
            pltpu.VMEM((7, T, H), BF16),
            pltpu.VMEM((7, T, H), BF16),
            pltpu.VMEM((2, T, H), BF16),
            pltpu.VMEM((2, T, H), BF16),
            pltpu.SemaphoreType.DMA((3,)),
            pltpu.SemaphoreType.DMA((COPIES,)),
            pltpu.SemaphoreType.DMA((COPIES,)),
        ],
        compiler_params=pltpu.CompilerParams(
            collective_id=0, has_side_effects=True, vmem_limit_bytes=62 * 2**20
        ),
    )(tokens, router, gate_up, down, shared_gate_up, shared_down, routes)


def running_sum(a):
    lower = jnp.tril(jnp.ones((a.shape[0], a.shape[0]), F32))
    return jnp.dot(lower, a, precision=highest)


def carried_in(part, axis, combine, identity, reverse):
    count = lax.axis_size(axis)
    place = lax.axis_index(axis)
    ahead = count - 1 - place if reverse else place
    gathered = jax.tree.map(lambda a: lax.all_gather(a, axis), part)
    state = jax.tree.map(lambda a, e: jnp.zeros_like(a) + jnp.asarray(e, a.dtype), part, identity)

    def one(turn, state):
        source = count - 1 - turn if reverse else turn
        return combine(
            state, jax.tree.map(lambda a: lax.dynamic_index_in_dim(a, source, 0, False), gathered)
        )

    return lax.fori_loop(0, ahead, one, state)


def document_index(starts, positions):
    return jnp.sum((starts[None, :] <= positions[:, None]).astype(jnp.int32), axis=1) - 1


def state_block(carry_state, block_inputs, decay_rate):
    values, step_sizes, write_half, read_half, documents, before = block_inputs
    writes = write_half.astype(jnp.float32)
    read_vectors = read_half.astype(jnp.float32)
    cumulative = running_sum(-step_sizes * decay_rate[None, :])
    token_order = jnp.arange(documents.shape[0], dtype=jnp.int32)
    causal = (documents[:, None] == documents[None, :]) & (
        token_order[:, None] >= token_order[None, :]
    )
    spread = cumulative.T[:, :, None] - cumulative.T[:, None, :]
    decayed = jnp.where(causal[None], jnp.exp(jnp.where(causal[None], spread, 0.0)), 0.0)
    affinity = jnp.einsum("tn,sn->ts", read_half, write_half, preferred_element_type=jnp.float32)
    weights = affinity[None] * decayed * step_sizes.T[:, None, :]
    output = jnp.einsum("hts,shp->thp", weights, values, precision=highest)
    carried = jnp.exp(cumulative) * (documents == before).astype(jnp.float32)[:, None]
    output = output + carried[:, :, None] * jnp.einsum(
        "hpn,tn->thp", carry_state, read_vectors, precision=highest
    )
    closing = (
        jnp.exp(cumulative[-1][None, :] - cumulative)
        * (documents == documents[-1]).astype(jnp.float32)[:, None]
        * step_sizes
    )
    keep_factor = jnp.exp(cumulative[-1]) * (documents[-1] == before).astype(jnp.float32)
    carry_state = keep_factor[:, None, None] * carry_state + jnp.einsum(
        "sh,shp,sn->hpn", closing, values, writes, precision=highest
    )
    return (carry_state, (output, weights, carried, closing, keep_factor))


def combine_states(earlier, later):
    return (earlier[0] * later[0], later[0][:, None, None] * earlier[1] + later[1])


def on_device(
    tokens,
    router,
    expert_gate_up,
    expert_down,
    shared_gate_up,
    shared_down,
    expert_index_table,
    document_length_table,
    step_sizes_unsoftened,
    state_input_vectors,
    state_output_vectors,
    decay_rate,
    skip_gain,
    cotangent,
):
    features = tokens[0]
    length = features.shape[0]
    model_width = features.shape[1]
    mixer_input_rows = routed_and_shared(
        tokens, router, expert_gate_up, expert_down, shared_gate_up, shared_down, expert_index_table
    )
    head_count = decay_rate.shape[0]
    head_dim = model_width // head_count
    state_size = state_input_vectors.shape[2]
    block_rows = min(128, length)
    block_count = length // block_rows
    values = mixer_input_rows.astype(jnp.float32).reshape(length, head_count, head_dim)
    step_sizes = jax.nn.softplus(step_sizes_unsoftened[0])
    writes = state_input_vectors[0].astype(jnp.float32)
    read_vectors = state_output_vectors[0].astype(jnp.float32)
    upstream = cotangent[0].astype(jnp.float32).reshape(length, head_count, head_dim)
    lengths_row = document_length_table[0]
    starts = jnp.cumsum(lengths_row) - lengths_row
    offset = lax.axis_index("ctx") * length
    positions = offset + jnp.arange(length, dtype=jnp.int32)
    documents = document_index(starts, positions)
    before = document_index(starts, positions - 1)
    block_writes = state_input_vectors[0].reshape(block_count, block_rows, state_size)
    block_reads = state_output_vectors[0].reshape(block_count, block_rows, state_size)
    inputs = (
        values.reshape(block_count, block_rows, head_count, head_dim),
        step_sizes.reshape(block_count, block_rows, head_count),
        block_writes,
        block_reads,
        documents.reshape(block_count, block_rows),
        before.reshape(block_count, block_rows)[:, 0],
    )

    def advance(carry_state, block_inputs):
        return state_block(carry_state, block_inputs, decay_rate)

    initial = jnp.zeros((head_count, head_dim, state_size), jnp.float32)
    local_state, (outputs, weights, carried, closing, keep_factor) = lax.scan(
        advance, initial, inputs
    )

    def retreat(grad_state, block_inputs):
        weight_block, seed_block, carry_weight, close_weight, keep_block, write_half, read_half = (
            block_inputs
        )
        write_block = write_half.astype(jnp.float32)
        read_block = read_half.astype(jnp.float32)
        back_term = jnp.einsum("hts,thp->shp", weight_block, seed_block, precision=highest)
        back_term = back_term + close_weight[:, :, None] * jnp.einsum(
            "hpn,sn->shp", grad_state, write_block, precision=highest
        )
        grad_state = keep_block[:, None, None] * grad_state + jnp.einsum(
            "th,thp,tn->hpn", carry_weight, seed_block, read_block, precision=highest
        )
        return (grad_state, back_term)

    local_grad, back_terms = lax.scan(
        retreat,
        initial,
        (
            weights,
            upstream.reshape(block_count, block_rows, head_count, head_dim),
            carried,
            closing,
            keep_factor,
            block_writes,
            block_reads,
        ),
        reverse=True,
    )
    cumulative = running_sum(-step_sizes * decay_rate[None, :])
    keep_all = jnp.exp(cumulative[-1]) * (documents[-1] == before[0]).astype(jnp.float32)
    identity = (jnp.ones_like(keep_all), jnp.zeros_like(local_state))
    entering = carried_in((keep_all, local_state), "ctx", combine_states, identity, False)[1]
    leaving = carried_in((keep_all, local_grad), "ctx", combine_states, identity, True)[1]
    entry_weight = jnp.exp(cumulative) * (documents == before[0]).astype(jnp.float32)[:, None]
    exit_weight = (
        jnp.exp(cumulative[-1][None, :] - cumulative)
        * (documents == documents[-1]).astype(jnp.float32)[:, None]
        * step_sizes
    )
    result = outputs.reshape(length, head_count, head_dim)
    result = result + entry_weight[:, :, None] * jnp.einsum(
        "hpn,tn->thp", entering, read_vectors, precision=highest
    )
    result = result + skip_gain[None, :, None] * values
    gradient = back_terms.reshape(length, head_count, head_dim)
    gradient = gradient + exit_weight[:, :, None] * jnp.einsum(
        "hpn,sn->shp", leaving, writes, precision=highest
    )
    gradient = gradient + skip_gain[None, :, None] * upstream
    return (
        result.reshape(1, length, model_width).astype(jnp.bfloat16),
        gradient.reshape(1, length, model_width).astype(jnp.bfloat16),
    )


def solution(mesh):
    return jax.shard_map(
        on_device,
        mesh=mesh,
        in_specs=(
            P("exp", "ctx", None),
            P(),
            P("exp", "ctx", None),
            P("exp", "ctx", None),
            P(),
            P(),
            P("exp", "ctx", None),
            P("exp", None),
            P("exp", "ctx", None),
            P("exp", "ctx", None),
            P("exp", "ctx", None),
            P(),
            P(),
            P("exp", "ctx", None),
        ),
        out_specs=(P("exp", "ctx", None), P("exp", "ctx", None)),
        check_vma=False,
    )
```

```python
import functools

import jax
import jax.numpy as jnp
from jax import lax
from jax.experimental import pallas as pl
from jax.experimental.pallas import tpu as pltpu
from jax.sharding import PartitionSpec as P

highest = lax.Precision.HIGHEST
MESH = pl.DeviceIdType.MESH
F32 = jnp.float32
BF16 = jnp.bfloat16

T = 128
D = 2560
E = 64
K = 8
FH = 256
NZ, NX, NY = 8, 4, 4
GR = D // 8
DR = FH // 8
HEADS = 40
N = 128
Q = D // 4
NEG = -1e30
SLOT = {4: 0, 3: 1, -3: 2, 2: 3, -2: 4, 1: 5, -1: 6, 0: 7}


def head_columns(first, count):
    h = lax.broadcasted_iota(jnp.int32, (N, count), 0)
    c = lax.broadcasted_iota(jnp.int32, (N, count), 1) + first
    return jnp.where((c >= h * 64) & (c < h * 64 + 64), 1.0, 0.0).astype(BF16)


def spread_heads(a, first, count):
    pick = head_columns(first, count)
    hi = a.astype(BF16)
    lo = (a - hi.astype(F32)).astype(BF16)
    return jnp.dot(hi, pick, preferred_element_type=F32) + jnp.dot(lo, pick, preferred_element_type=F32)


def kernel(
    x_hbm, router_ref, gu_hbm, dn_hbm, sgu_hbm, sdn_hbm, idx_ref, len_ref, raw_ref, b_ref, c_ref,
    rate_ref, skip_ref, cot_ref, out_ref, grad_ref,
    xall, gall, wg, wd, hid, part, shared, rr, rl, sr, sl_,
    cum, cumt, dt, dtt, aff, same, bt, ct, carried, closing, wmat, keeps, kown, ksib, skips, intra,
    lown, lsib, town, tin, sown, sin, lownb, lsibb, townb, tinb, sownb, sinb,
    loc, ss, rs,
):
    ctx = lax.axis_index("ctx")
    exp = lax.axis_index("exp")
    z, x = exp // NX, exp % NX
    y, core = ctx // 2, ctx % 2
    zp = {"exp": (exp + NX) % (NX * NZ)}
    zm = {"exp": (exp + NX * (NZ - 1)) % (NX * NZ)}
    xp = {"exp": z * NX + (x + 1) % NX}
    xm = {"exp": z * NX + (x + NX - 1) % NX}
    yp = {"ctx": (ctx + 2) % 8}
    ym = {"ctx": (ctx + 6) % 8}
    sib = {"ctx": ctx + 1 - 2 * core}
    y1, y2, y3 = (y + 1) % NY, (y + 2) % NY, (y + 3) % NY
    other = 1 - core

    counter = [0]

    def rcopy(src, dst, dev, k):
        return pltpu.make_async_remote_copy(
            src_ref=src, dst_ref=dst, send_sem=ss.at[k], recv_sem=rs.at[k],
            device_id=dev, device_id_type=MESH,
        )

    sent = []

    def send(src, dst, dev):
        k = counter[0]
        counter[0] += 1
        c = rcopy(src, dst, dev, k)
        c.start()
        sent.append(c)
        return k

    def arrived(k, region):
        rcopy(region, region, sib, k).wait_recv()

    barrier = pltpu.get_barrier_semaphore()
    for dev in (zp, zm, xp, xm, yp, ym, sib):
        pl.semaphore_signal(barrier, inc=1, device_id=dev, device_id_type=MESH)

    x_own = xall.at[SLOT[0]]
    lx = pltpu.make_async_copy(x_hbm.at[0], x_own, loc.at[0])
    lx.start()
    SG, SU, SD = 0, D, 2 * D
    shared_copies = [
        pltpu.make_async_copy(sgu_hbm.at[:, pl.ds(0, FH)], hid.at[pl.ds(SG, D)], loc.at[3]),
        pltpu.make_async_copy(sgu_hbm.at[:, pl.ds(FH, FH)], hid.at[pl.ds(SU, D)], loc.at[4]),
    ] + [
        pltpu.make_async_copy(
            sdn_hbm.at[:, pl.ds(i * FH, FH)], hid.at[pl.ds(SD + i * FH, FH)], loc.at[5 + i]
        )
        for i in range(D // FH)
    ]
    for c in shared_copies:
        c.start()
    pl.semaphore_wait(barrier, 7)

    kx = {}
    kx[-1] = send(x_hbm.at[0], xall.at[SLOT[-1]], zp)
    kx[1] = send(x_hbm.at[0], xall.at[SLOT[1]], zm)

    HC = D // 2
    parts = {"g": (gu_hbm, wg, GR, None), "d0": (dn_hbm, wd, DR, pl.ds(0, HC)), "d1": (dn_hbm, wd, DR, pl.ds(HC, HC))}

    def region(name, slot, e, yy, cc, rows=slice(None)):
        w, cols = parts[name][1], parts[name][3]
        return w.at[slot, e, yy, cc, rows] if cols is None else w.at[slot, e, yy, cc, rows, cols]

    def mine(name, e):
        w, cols = parts[name][0], parts[name][3]
        if e is None:
            return w if cols is None else w.at[:, :, cols]
        return w.at[e] if cols is None else w.at[e, :, cols]

    key = {}
    every = slice(None)

    def zeroth(name):
        key[name, "A", 2] = send(mine(name, 0), region(name, 2, 0, y, core), xp)
        key[name, "A", 1] = send(mine(name, 0), region(name, 1, 0, y, core), xm)
        key[name, "B", 3] = send(mine(name, 1), region(name, 0, 1, y, core), yp)
        key[name, "B", 1] = send(mine(name, 1), region(name, 0, 1, y, core), ym)
        key[name, "S"] = send(mine(name, None), region(name, 0, every, y, core), sib)

    def first_ring(name):
        h = parts[name][2] // 2
        lo_, hi_ = pl.ds(0, h), pl.ds(h, h)
        arrived(key[name, "A", 2], region(name, 2, 0, y, core))
        key[name, "hA", 2] = send(region(name, 2, 0, y, core, lo_), region(name, 3, 0, y, core, lo_), xp)
        arrived(key[name, "A", 1], region(name, 1, 0, y, core))
        key[name, "hA", 1] = send(region(name, 1, 0, y, core, hi_), region(name, 3, 0, y, core, hi_), xm)
        b3, b1 = region(name, 0, 1, y3, core), region(name, 0, 1, y1, core)
        arrived(key[name, "B", 3], b3)
        key[name, "hB", 3] = send(region(name, 0, 1, y3, core, lo_), region(name, 0, 1, y3, core, lo_), yp)
        arrived(key[name, "B", 1], b1)
        key[name, "hB", 1] = send(region(name, 0, 1, y1, core, hi_), region(name, 0, 1, y1, core, hi_), ym)
        key[name, "B3S"] = send(b3, b3, sib)
        key[name, "B1S"] = send(b1, b1, sib)

    def second_ring(name):
        h = parts[name][2] // 2
        lo_, hi_ = pl.ds(0, h), pl.ds(h, h)
        arrived(key[name, "hA", 2], region(name, 3, 0, y, core, lo_))
        arrived(key[name, "hA", 1], region(name, 3, 0, y, core, hi_))
        a = region(name, every, 0, y, core)
        key[name, "sA", 3] = send(a, a, yp)
        key[name, "sA", 1] = send(a, a, ym)
        arrived(key[name, "hB", 3], region(name, 0, 1, y2, core, lo_))
        arrived(key[name, "hB", 1], region(name, 0, 1, y2, core, hi_))
        b = region(name, 0, 1, every, core)
        key[name, "sB", 2] = send(b, region(name, 2, 1, every, core), xp)
        key[name, "sB", 1] = send(b, region(name, 1, 1, every, core), xm)
        s = region(name, 0, 1, y2, core)
        key[name, "B2S"] = send(s, s, sib)
        s = region(name, pl.ds(1, 3), 0, y, core)
        key[name, "AS"] = send(s, s, sib)

    def third(name):
        b2, b1 = region(name, 2, 1, every, core), region(name, 1, 1, every, core)
        arrived(key[name, "sB", 2], b2)
        two = pl.ds(0, 2)
        key[name, "lB", 2] = send(region(name, 2, 1, two, core), region(name, 3, 1, two, core), xp)
        arrived(key[name, "sB", 1], b1)
        two = pl.ds(2, 2)
        key[name, "lB", 1] = send(region(name, 1, 1, two, core), region(name, 3, 1, two, core), xm)
        a3, a1 = region(name, every, 0, y3, core), region(name, every, 0, y1, core)
        arrived(key[name, "sA", 3], a3)
        s = region(name, pl.ds(0, 2), 0, y3, core)
        key[name, "lA", 3] = send(s, s, yp)
        arrived(key[name, "sA", 1], a1)
        s = region(name, pl.ds(2, 2), 0, y1, core)
        key[name, "lA", 1] = send(s, s, ym)
        for k, s in (("tB2", b2), ("tB1", b1), ("tA3", a3), ("tA1", a1)):
            key[name, k] = send(s, s, sib)

    def fourth(name):
        arrived(key[name, "lA", 3], region(name, pl.ds(0, 2), 0, y2, core))
        arrived(key[name, "lA", 1], region(name, pl.ds(2, 2), 0, y2, core))
        s = region(name, every, 0, y2, core)
        key[name, "fA"] = send(s, s, sib)
        arrived(key[name, "lB", 2], region(name, 3, 1, pl.ds(0, 2), core))
        arrived(key[name, "lB", 1], region(name, 3, 1, pl.ds(2, 2), core))
        s = region(name, 3, 1, every, core)
        key[name, "fB"] = send(s, s, sib)

    def sibling_first(name):
        arrived(key[name, "S"], region(name, 0, every, y, other))
        arrived(key[name, "B3S"], region(name, 0, 1, y3, other))
        arrived(key[name, "B1S"], region(name, 0, 1, y1, other))
        arrived(key[name, "B2S"], region(name, 0, 1, y2, other))

    def sibling_third(name):
        arrived(key[name, "tB2"], region(name, 2, 1, every, other))
        arrived(key[name, "tB1"], region(name, 1, 1, every, other))

    def sibling_last(name):
        arrived(key[name, "AS"], region(name, pl.ds(1, 3), 0, y, other))
        arrived(key[name, "tA3"], region(name, every, 0, y3, other))
        arrived(key[name, "tA1"], region(name, every, 0, y1, other))
        arrived(key[name, "fA"], region(name, every, 0, y2, other))
        arrived(key[name, "fB"], region(name, 3, 1, every, other))

    for name in ("g", "d0", "d1"):
        zeroth(name)
    lg = pltpu.make_async_copy(gu_hbm, wg.at[0, :, y, core], loc.at[1])
    ld = pltpu.make_async_copy(dn_hbm, wd.at[0, :, y, core], loc.at[2])
    lg.start()
    ld.start()

    lx.wait()
    xo = x_own[...]
    logits = jnp.dot(xo, router_ref[...], preferred_element_type=F32)
    lane = lax.broadcasted_iota(jnp.int32, (T, E), 1)
    chosen = jnp.zeros((T, E), F32)
    idx = idx_ref[0]
    for j in range(K):
        chosen = chosen + jnp.where(idx[:, j : j + 1] == lane, 1.0, 0.0)
    sig = chosen * jax.nn.sigmoid(logits)
    gate = sig / jnp.sum(sig, axis=1, keepdims=True)
    hi = gate.astype(BF16)
    lo = (gate - hi.astype(F32)).astype(BF16)
    gall[SLOT[0], :, 0:E] = hi
    gall[SLOT[0], :, E : 2 * E] = lo
    kg = {}
    kg[-1] = send(gall.at[SLOT[0]], gall.at[SLOT[-1]], zp)
    kg[1] = send(gall.at[SLOT[0]], gall.at[SLOT[1]], zm)

    def shared_expert():
        for c in shared_copies:
            c.wait()
        xo = x_own[...]
        sa = jnp.dot(xo, hid[SG : SG + D], preferred_element_type=F32)
        sb = jnp.dot(xo, hid[SU : SU + D], preferred_element_type=F32)
        sh = (jax.nn.silu(sa) * sb).astype(BF16)
        for i in range(D // FH):
            cols = slice(i * FH, (i + 1) * FH)
            shared[:, cols] = xo[:, cols].astype(F32) + jnp.dot(
                sh, hid[SD + i * FH : SD + (i + 1) * FH], preferred_element_type=F32
            )

    def token_step(d):
        for buf, keys in ((xall, kx), (gall, kg)):
            arrived(keys[-d], buf.at[SLOT[-d]])
            arrived(keys[d], buf.at[SLOT[d]])
            if d < 3:
                keys[-d - 1] = send(buf.at[SLOT[-d]], buf.at[SLOT[-d - 1]], zp)
                keys[d + 1] = send(buf.at[SLOT[d]], buf.at[SLOT[d + 1]], zm)
            else:
                lo_, hi_ = pl.ds(0, T // 2), pl.ds(T // 2, T // 2)
                keys["lo"] = send(buf.at[SLOT[-3], lo_], buf.at[SLOT[4], lo_], zp)
                keys["hi"] = send(buf.at[SLOT[3], hi_], buf.at[SLOT[4], hi_], zm)

    row_i = lax.broadcasted_iota(jnp.int32, (T, T), 0)
    col_i = lax.broadcasted_iota(jnp.int32, (T, T), 1)
    second_f = core == 1
    second_b = core == 0

    def decays():
        dt[...] = jnp.zeros((T, N), F32)
        cum[...] = jnp.zeros((T, N), F32)
        steps = jax.nn.softplus(raw_ref[0])
        dt[:, 0:HEADS] = steps
        cum[:, 0:HEADS] = -steps * rate_ref[...]
        lower = jnp.where(row_i >= col_i, 1.0, 0.0)
        c = jnp.dot(lower, cum[...], precision=highest, preferred_element_type=F32)
        cum[...] = c
        cumt[...] = c.T
        dtt[...] = dt[...].T
        b, cc = b_ref[0], c_ref[0]
        bt[...] = b.astype(F32).T.astype(BF16)
        ct[...] = cc.astype(F32).T.astype(BF16)
        lens = jnp.broadcast_to(len_ref[...].astype(F32), (8, 8))
        before = lax.broadcasted_iota(jnp.int32, (8, 8), 1) < lax.broadcasted_iota(jnp.int32, (8, 8), 0)
        starts = jnp.sum(jnp.where(before, lens, 0.0), axis=1, keepdims=True)
        offset = (ctx * T).astype(F32)
        place = lax.broadcasted_iota(jnp.int32, (8, T), 1).astype(F32) + offset

        def number(p):
            return jnp.sum(jnp.where(starts <= p, 1.0, 0.0), axis=0, keepdims=True)

        doc_row = jnp.broadcast_to(number(place), (T, T))
        doc_col = doc_row.T
        ahead = jnp.broadcast_to(number(place[:, 0:1] - 1.0), (T, T))
        final = jnp.broadcast_to(number(place[:, T - 1 : T]), (T, T))
        same[...] = jnp.where(doc_row == doc_col, 1.0, 0.0)
        end = c[T - 1 : T, :]
        carry = jnp.exp(c) * jnp.where(doc_col == ahead, 1.0, 0.0)
        close = jnp.exp(end - c) * jnp.where(doc_col == final, 1.0, 0.0) * dt[...]
        keep = jnp.exp(end) * jnp.where(final[0:1] == ahead[0:1], 1.0, 0.0)
        keeps[0] = jnp.broadcast_to(keep, (8, N))
        key["keep"] = send(keeps.at[0], keeps.at[1], sib)
        skip = jnp.concatenate([skip_ref[...], jnp.zeros((1, N - HEADS), F32)], axis=1)
        for i in range(4):
            cols = slice(i * Q, (i + 1) * Q)
            carried[:, cols] = spread_heads(carry, i * Q, Q)
            closing[:, cols] = spread_heads(close, i * Q, Q)
            skips[:, cols] = spread_heads(jnp.broadcast_to(skip, (8, N)), i * Q, Q)
            kown[:, cols] = spread_heads(keeps[0], i * Q, Q)
        aff[...] = lax.dot_general(cc, b, (((1,), (1,)), ((), ())), preferred_element_type=F32)

    def column(a, h):
        return jnp.sum(jnp.where(col_i == h, a, 0.0), axis=1, keepdims=True)

    def forward_weights():
        causal = (same[...] > 0.5) & (row_i >= col_i)
        a = aff[...]
        c = cum[...]

        def pair(p, _):
            for j in range(2):
                h = 2 * p + j
                gap = column(c, h) - cumt[pl.ds(h, 1), :]
                w = a * jnp.exp(jnp.where(causal, gap, NEG)) * dtt[pl.ds(h, 1), :]
                wmat[p, j * T : (j + 1) * T, :] = w.astype(BF16)
            return 0

        lax.fori_loop(0, HEADS // 2, pair, 0)

    def gradient_states():
        for i in range(4):
            cols = slice(i * Q, (i + 1) * Q)
            v = (carried[:, cols] * cot_ref[0, :, cols].astype(F32)).astype(BF16)
            lownb[:, cols] = jnp.dot(ct[...], v, preferred_element_type=F32).astype(BF16)
        key["lb"] = send(lownb, lsibb, sib)
        arrived(key["keep"], keeps.at[1])
        for i in range(4):
            cols = slice(i * Q, (i + 1) * Q)
            ksib[:, cols] = spread_heads(keeps[1], i * Q, Q)

    rows_own = pl.ds(pl.multiple_of(core * 64, 64), 64)
    rows_other = pl.ds(pl.multiple_of(other * 64, 64), 64)

    def chip_state(cols, lo_, ls, to, second):
        ko, ks = kown[0:1, cols], ksib[0:1, cols]
        one = jnp.ones_like(ko)
        t = jnp.where(second, one, ks) * lo_[rows_own, cols].astype(F32)
        t = t + jnp.where(second, ko, one) * ls[rows_own, cols].astype(F32)
        to[:, cols] = t.astype(BF16)

    def passed_on(cols, to, ti, so):
        k = kown[0:1, cols] * ksib[0:1, cols]
        so[:, cols] = (to[:, cols].astype(F32) + k * ti[:, cols].astype(F32)).astype(BF16)

    def entering(cols, ls, si, second):
        ks = ksib[0:1, cols]
        s = jnp.where(second, ks, jnp.ones_like(ks)) * si[:, cols].astype(F32)
        s = s + jnp.where(second, 1.0, 0.0) * ls[:, cols].astype(F32)
        return s.astype(BF16)

    def gradient_one():
        arrived(key["lb"], lsibb)
        for i in range(4):
            chip_state(slice(i * Q, (i + 1) * Q), lownb, lsibb, townb, second_b)
        key["tb"] = send(townb, tinb, ym)

    def gradient_two():
        arrived(key["tb"], tinb)
        for i in range(4):
            passed_on(slice(i * Q, (i + 1) * Q), townb, tinb, sownb)
        key["sb"] = send(sownb, sinb.at[rows_own], ym)

    def gradient_three():
        arrived(key["sb"], sinb.at[rows_own])
        key["ob"] = send(sinb.at[rows_own], sinb.at[rows_own], sib)

    def gradient_four():
        arrived(key["ob"], sinb.at[rows_other])
        causal = (same[...] > 0.5) & (row_i <= col_i)
        b = b_ref[0]
        a = lax.dot_general(b, c_ref[0], (((1,), (1,)), ((), ())), preferred_element_type=F32)
        c = cum[...]
        d = dt[...]
        left = col_i < 64

        def pair(p, _):
            cols = pl.ds(pl.multiple_of(p * N, N), N)
            seed = cot_ref[0, :, cols]
            halves = []
            for j in range(2):
                h = 2 * p + j
                gap = cumt[pl.ds(h, 1), :] - column(c, h)
                w = a * jnp.exp(jnp.where(causal, gap, NEG)) * column(d, h)
                halves.append(jnp.dot(w.astype(BF16), seed, preferred_element_type=F32))
            g = jnp.where(left, halves[0], halves[1])
            s = entering(cols, lsibb, sinb, second_b)
            g = g + closing[:, cols] * jnp.dot(b, s, preferred_element_type=F32)
            g = g + skips[0:1, cols] * seed.astype(F32)
            grad_ref[0, :, cols] = g.astype(BF16)
            return 0

        lax.fori_loop(0, HEADS // 2, pair, 0)

    def forward_zero(q, u):
        cols = slice(q * Q, (q + 1) * Q)
        v = (closing[:, cols] * u.astype(F32)).astype(BF16)
        lown[:, cols] = jnp.dot(bt[...], v, preferred_element_type=F32).astype(BF16)
        key["l", q] = send(lown.at[:, cols], lsib.at[:, cols], sib)
        left = col_i < 64
        for i in range(Q // N):
            p = q * (Q // N) + i
            pc = slice(p * N, (p + 1) * N)
            up = u[:, i * N : (i + 1) * N]
            r = jnp.dot(wmat[p], up, preferred_element_type=F32)
            intra[:, pc] = jnp.where(left, r[0:T], r[T:]) + skips[0:1, pc] * up.astype(F32)

    def forward_one(q):
        cols = slice(q * Q, (q + 1) * Q)
        arrived(key["l", q], lsib.at[:, cols])
        chip_state(cols, lown, lsib, town, second_f)
        key["t", q] = send(town.at[:, cols], tin.at[:, cols], yp)

    def forward_two(q):
        cols = slice(q * Q, (q + 1) * Q)
        arrived(key["t", q], tin.at[:, cols])
        passed_on(cols, town, tin, sown)
        key["s", q] = send(sown.at[:, cols], sin.at[rows_own, cols], yp)

    def forward_three(q):
        cols = slice(q * Q, (q + 1) * Q)
        arrived(key["s", q], sin.at[rows_own, cols])
        key["o", q] = send(sin.at[rows_own, cols], sin.at[rows_own, cols], sib)

    def forward_four(q):
        cols = slice(q * Q, (q + 1) * Q)
        arrived(key["o", q], sin.at[rows_other, cols])
        s = entering(cols, lsib, sin, second_f)
        r = intra[:, cols] + carried[:, cols] * jnp.dot(c_ref[0], s, preferred_element_type=F32)
        out_ref[0, :, cols] = r.astype(BF16)

    MT = 256

    def hidden_tile(n, m):
        slot, e = n // 2, n % 2
        away = jnp.where(slot == 2, 3, jnp.where(slot == 3, 2, slot))
        expert = 2 * (z * NX + (x + away) % NX) + e
        r = lax.broadcasted_iota(jnp.int32, (2 * E, FH), 0)
        sel = jnp.where((r == expert) | (r == expert + E), 1.0, 0.0).astype(BF16)
        xs = xall[pl.ds(m * (MT // T), MT // T)].reshape(MT, D)
        gs = gall[pl.ds(m * (MT // T), MT // T)].reshape(MT, 2 * E)
        w = wg[slot, e].reshape(D, 2 * FH)
        p = jnp.dot(xs, w, preferred_element_type=F32)
        g = jnp.dot(gs, sel, preferred_element_type=F32)
        h = (jax.nn.silu(p[:, :FH]) * p[:, FH:] * g).astype(BF16)
        hid[pl.ds(pl.multiple_of(n * NZ * T + m * MT, MT), MT), :] = h

    def hidden(experts, tiles):
        def one(i, _):
            hidden_tile(experts[0] + experts[1] * (i // tiles[1]), tiles[0] + i % tiles[1])
            return 0

        lax.fori_loop(0, experts[2] * tiles[1], one, 0)

    NC = 256

    def partial(first, rows, hf, into):
        def tile(c, _):
            cols = pl.ds(pl.multiple_of(hf * HC + c * NC, NC), NC)
            acc = jnp.zeros((rows, NC), F32)
            for n in range(8):
                acc = acc + jnp.dot(
                    hid[pl.ds(n * NZ * T + first * T, rows), :],
                    wd[n // 2, n % 2, :, :, :, cols].reshape(FH, NC),
                    preferred_element_type=F32,
                )
            if into is part:
                part[pl.ds(0, rows), pl.ds(pl.multiple_of(c * NC, NC), NC)] = acc
            else:
                into[:, cols] += acc
            return 0

        lax.fori_loop(0, HC // NC, tile, 0)

    kr, kl = {}, {}
    c0, c1 = slice(0, Q), slice(Q, 2 * Q)

    def scatter_start(hf):
        partial(SLOT[4], T, hf, part)
        sr[hf, 0] = part[0:T, c0].astype(BF16)
        kr[hf, 0] = send(sr.at[hf, 0], rr.at[hf, 0], zp)
        sl_[hf, 0] = part[0:T, c1].astype(BF16)
        kl[hf, 0] = send(sl_.at[hf, 0], rl.at[hf, 0], zm)
        partial(SLOT[3], 2 * T, hf, part)
        sr[hf, 1] = part[0:T, c1].astype(BF16)
        kr[hf, 1] = send(sr.at[hf, 1], rr.at[hf, 1], zp)
        sl_[hf, 1] = part[T : 2 * T, c0].astype(BF16)
        kl[hf, 1] = send(sl_.at[hf, 1], rl.at[hf, 1], zm)

    def relay(hf, k):
        cr, cl = (c0, c1) if k % 2 == 0 else (c1, c0)
        arrived(kr[hf, k], rr.at[hf, k])
        rr[hf, k] = (rr[hf, k].astype(F32) + part[0:T, cr]).astype(BF16)
        kr[hf, k + 2] = send(rr.at[hf, k], rr.at[hf, k + 2], zp)
        arrived(kl[hf, k], rl.at[hf, k])
        rl[hf, k] = (rl[hf, k].astype(F32) + part[T : 2 * T, cl]).astype(BF16)
        kl[hf, k + 2] = send(rl.at[hf, k], rl.at[hf, k + 2], zm)

    def mixer_in(hf):
        for k in (5, 6):
            arrived(kr[hf, k], rr.at[hf, k])
            arrived(kl[hf, k], rl.at[hf, k])
        for i, (a, b) in enumerate(((6, 5), (5, 6))):
            q = 2 * hf + i
            cols = slice(q * Q, (q + 1) * Q)
            u = shared[:, cols] + rr[hf, a].astype(F32) + rl[hf, b].astype(F32)
            forward_zero(q, u.astype(BF16))

    shared_expert()
    decays()
    gradient_states()
    lg.wait()
    ld.wait()
    first_ring("g")
    second_ring("g")
    token_step(1)
    first_ring("d0")
    first_ring("d1")
    forward_weights()
    sibling_first("g")
    hidden((1, 2, 1), (3, 1))
    token_step(2)
    hidden((1, 2, 1), (2, 1))
    third("g")
    token_step(3)
    second_ring("d0")
    second_ring("d1")
    sibling_third("g")
    hidden((3, 2, 2), (2, 2))
    hidden((1, 2, 3), (1, 1))
    for buf, keys in ((xall, kx), (gall, kg)):
        arrived(keys["lo"], buf.at[SLOT[4], pl.ds(0, T // 2)])
        arrived(keys["hi"], buf.at[SLOT[4], pl.ds(T // 2, T // 2)])
    fourth("g")
    hidden((1, 2, 3), (0, 1))
    sibling_last("g")
    hidden((0, 2, 2), (0, 4))
    third("d0")
    hidden((4, 2, 2), (0, 4))
    hidden((7, 2, 1), (0, 4))
    third("d1")
    fourth("d0")
    sibling_first("d0")
    sibling_third("d0")
    sibling_last("d0")
    scatter_start(0)
    relay(0, 0)
    partial(SLOT[2], 2 * T, 0, part)
    fourth("d1")
    relay(0, 1)
    relay(0, 2)
    partial(SLOT[1], 2 * T, 0, part)
    relay(0, 3)
    relay(0, 4)
    sibling_first("d1")
    sibling_third("d1")
    sibling_last("d1")
    scatter_start(1)
    partial(SLOT[0], T, 0, shared)
    mixer_in(0)
    relay(1, 0)
    partial(SLOT[2], 2 * T, 1, part)
    gradient_one()
    forward_one(0)
    forward_one(1)
    relay(1, 1)
    relay(1, 2)
    partial(SLOT[1], 2 * T, 1, part)
    gradient_two()
    forward_two(0)
    forward_two(1)
    relay(1, 3)
    relay(1, 4)
    partial(SLOT[0], T, 1, shared)
    forward_three(0)
    forward_three(1)
    gradient_three()
    gradient_four()
    forward_four(0)
    forward_four(1)
    mixer_in(1)
    for stage in (forward_one, forward_two, forward_three, forward_four):
        stage(2)
        stage(3)
    for c in sent:
        c.wait_send()


COPIES = 2 + 3 * 27 + 2 + 12 + 28 + 1 + 4 + 16


def on_device(
    tokens, router, gate_up, down, shared_gate_up, shared_down, routes, lengths,
    steps, writes, reads, decay_rate, skip_gain, cotangent,
):
    vmem = pl.BlockSpec(memory_space=pltpu.VMEM)
    hbm = pl.BlockSpec(memory_space=pl.ANY)
    wide = pltpu.VMEM((T, D), F32)
    square = pltpu.VMEM((T, N), F32)
    small = pltpu.VMEM((N, N), BF16)
    state = pltpu.VMEM((N, D), BF16)
    half = pltpu.VMEM((N // 2, D), BF16)
    row = pltpu.VMEM((8, D), F32)
    return pl.pallas_call(
        kernel,
        out_shape=[jax.ShapeDtypeStruct((1, T, D), BF16)] * 2,
        in_specs=[hbm, vmem, hbm, hbm, hbm, hbm] + [vmem] * 8,
        out_specs=[vmem, vmem],
        scratch_shapes=[
            pltpu.VMEM((NZ, T, D), BF16),
            pltpu.VMEM((NZ, T, 2 * E), BF16),
            pltpu.VMEM((NX, 2, NY, 2, GR, 2 * FH), BF16),
            pltpu.VMEM((NX, 2, NY, 2, DR, D), BF16),
            pltpu.VMEM((NX * 2 * NZ * T, FH), BF16),
            pltpu.VMEM((2 * T, 2 * Q), F32),
            wide,
            pltpu.VMEM((2, 7, T, Q), BF16),
            pltpu.VMEM((2, 7, T, Q), BF16),
            pltpu.VMEM((2, 2, T, Q), BF16),
            pltpu.VMEM((2, 2, T, Q), BF16),
            square, square, square, square, square, square, small, small, wide, wide,
            pltpu.VMEM((HEADS // 2, 2 * T, T), BF16),
            pltpu.VMEM((2, 8, N), F32),
            row, row, row, wide,
            state, state, half, half, half, state,
            state, state, half, half, half, state,
            pltpu.SemaphoreType.DMA((5 + D // FH,)),
            pltpu.SemaphoreType.DMA((COPIES,)),
            pltpu.SemaphoreType.DMA((COPIES,)),
        ],
        compiler_params=pltpu.CompilerParams(
            collective_id=0, has_side_effects=True, vmem_limit_bytes=63 * 2**20
        ),
    )(
        tokens, router, gate_up, down, shared_gate_up, shared_down, routes, lengths,
        steps, writes, reads, decay_rate.reshape(1, -1), skip_gain.reshape(1, -1), cotangent,
    )


def solution(mesh):
    return jax.shard_map(
        on_device,
        mesh=mesh,
        in_specs=(
            P("exp", "ctx", None),
            P(),
            P("exp", "ctx", None),
            P("exp", "ctx", None),
            P(),
            P(),
            P("exp", "ctx", None),
            P("exp", None),
            P("exp", "ctx", None),
            P("exp", "ctx", None),
            P("exp", "ctx", None),
            P(),
            P(),
            P("exp", "ctx", None),
        ),
        out_specs=(P("exp", "ctx", None), P("exp", "ctx", None)),
        check_vma=False,
    )
```

```python
import functools

import jax
import jax.numpy as jnp
from jax import lax
from jax.experimental import pallas as pl
from jax.experimental.pallas import tpu as pltpu
from jax.sharding import PartitionSpec as P

highest = lax.Precision.HIGHEST
MESH = pl.DeviceIdType.MESH
F32 = jnp.float32
BF16 = jnp.bfloat16

T = 128
D = 2560
E = 64
K = 8
FH = 256
NZ, NX, NY = 8, 4, 4
GR = D // 8
DR = FH // 8
HEADS = 40
N = 128
Q = D // 4
NEG = -1e30
SLOT = {4: 0, 3: 1, -3: 2, 2: 3, -2: 4, 1: 5, -1: 6, 0: 7}


def head_columns(first, count):
    h = lax.broadcasted_iota(jnp.int32, (N, count), 0)
    c = lax.broadcasted_iota(jnp.int32, (N, count), 1) + first
    return jnp.where((c >= h * 64) & (c < h * 64 + 64), 1.0, 0.0).astype(BF16)


def spread_heads(a, first, count):
    pick = head_columns(first, count)
    hi = a.astype(BF16)
    lo = (a - hi.astype(F32)).astype(BF16)
    return jnp.dot(hi, pick, preferred_element_type=F32) + jnp.dot(lo, pick, preferred_element_type=F32)


def kernel(
    x_hbm, router_ref, gu_hbm, dn_hbm, sgu_hbm, sdn_hbm, idx_ref, len_ref, raw_ref, b_ref, c_ref,
    rate_ref, skip_ref, cot_ref, out_ref, grad_ref,
    xall, gall, wg, wd, hid, part, shared, rr, rl, sr, sl_,
    cum, cumt, dt, dtt, aff, same, bt, ct, carried, closing, wmat, keeps, kown, ksib, skips, intra,
    lown, lsib, town, tin, sown, sin, lownb, lsibb, townb, tinb, sownb, sinb,
    loc, ss, rs,
):
    ctx = lax.axis_index("ctx")
    exp = lax.axis_index("exp")
    z, x = exp // NX, exp % NX
    y, core = ctx // 2, ctx % 2
    zp = {"exp": (exp + NX) % (NX * NZ)}
    zm = {"exp": (exp + NX * (NZ - 1)) % (NX * NZ)}
    xp = {"exp": z * NX + (x + 1) % NX}
    xm = {"exp": z * NX + (x + NX - 1) % NX}
    yp = {"ctx": (ctx + 2) % 8}
    ym = {"ctx": (ctx + 6) % 8}
    sib = {"ctx": ctx + 1 - 2 * core}
    y1, y2, y3 = (y + 1) % NY, (y + 2) % NY, (y + 3) % NY
    other = 1 - core

    counter = [0]

    def rcopy(src, dst, dev, k):
        return pltpu.make_async_remote_copy(
            src_ref=src, dst_ref=dst, send_sem=ss.at[k], recv_sem=rs.at[k],
            device_id=dev, device_id_type=MESH,
        )

    sent = []

    def send(src, dst, dev):
        k = counter[0]
        counter[0] += 1
        c = rcopy(src, dst, dev, k)
        c.start()
        sent.append(c)
        return k

    def arrived(k, region):
        rcopy(region, region, sib, k).wait_recv()

    barrier = pltpu.get_barrier_semaphore()
    for dev in (zp, zm, xp, xm, yp, ym, sib):
        pl.semaphore_signal(barrier, inc=1, device_id=dev, device_id_type=MESH)

    x_own = xall.at[SLOT[0]]
    lx = pltpu.make_async_copy(x_hbm.at[0], x_own, loc.at[0])
    lx.start()
    SG, SU, SD = 0, D, 2 * D
    shared_copies = [
        pltpu.make_async_copy(sgu_hbm.at[:, pl.ds(0, FH)], hid.at[pl.ds(SG, D)], loc.at[3]),
        pltpu.make_async_copy(sgu_hbm.at[:, pl.ds(FH, FH)], hid.at[pl.ds(SU, D)], loc.at[4]),
    ] + [
        pltpu.make_async_copy(
            sdn_hbm.at[:, pl.ds(i * FH, FH)], hid.at[pl.ds(SD + i * FH, FH)], loc.at[5 + i]
        )
        for i in range(D // FH)
    ]
    for c in shared_copies:
        c.start()
    pl.semaphore_wait(barrier, 7)

    kx = {}
    kx[-1] = send(x_hbm.at[0], xall.at[SLOT[-1]], zp)
    kx[1] = send(x_hbm.at[0], xall.at[SLOT[1]], zm)

    HC = D // 2
    parts = {"g": (gu_hbm, wg, GR, None), "d0": (dn_hbm, wd, DR, pl.ds(0, HC)), "d1": (dn_hbm, wd, DR, pl.ds(HC, HC))}

    def region(name, slot, e, yy, cc, rows=slice(None)):
        w, cols = parts[name][1], parts[name][3]
        return w.at[slot, e, yy, cc, rows] if cols is None else w.at[slot, e, yy, cc, rows, cols]

    def mine(name, e):
        w, cols = parts[name][0], parts[name][3]
        if e is None:
            return w if cols is None else w.at[:, :, cols]
        return w.at[e] if cols is None else w.at[e, :, cols]

    key = {}
    every = slice(None)

    def zeroth(name):
        key[name, "A", 2] = send(mine(name, 0), region(name, 2, 0, y, core), xp)
        key[name, "A", 1] = send(mine(name, 0), region(name, 1, 0, y, core), xm)
        key[name, "B", 3] = send(mine(name, 1), region(name, 0, 1, y, core), yp)
        key[name, "B", 1] = send(mine(name, 1), region(name, 0, 1, y, core), ym)
        own = 1 if name == "g" else None
        key[name, "S"] = send(mine(name, own), region(name, 0, every if own is None else own, y, core), sib)

    def first_ring(name):
        h = parts[name][2] // 2
        lo_, hi_ = pl.ds(0, h), pl.ds(h, h)
        arrived(key[name, "A", 2], region(name, 2, 0, y, core))
        key[name, "hA", 2] = send(region(name, 2, 0, y, core, lo_), region(name, 3, 0, y, core, lo_), xp)
        arrived(key[name, "A", 1], region(name, 1, 0, y, core))
        key[name, "hA", 1] = send(region(name, 1, 0, y, core, hi_), region(name, 3, 0, y, core, hi_), xm)
        b3, b1 = region(name, 0, 1, y3, core), region(name, 0, 1, y1, core)
        arrived(key[name, "B", 3], b3)
        key[name, "hB", 3] = send(region(name, 0, 1, y3, core, lo_), region(name, 0, 1, y3, core, lo_), yp)
        arrived(key[name, "B", 1], b1)
        key[name, "hB", 1] = send(region(name, 0, 1, y1, core, hi_), region(name, 0, 1, y1, core, hi_), ym)
        key[name, "B3S"] = send(b3, b3, sib)
        key[name, "B1S"] = send(b1, b1, sib)

    def second_ring_a(name):
        h = parts[name][2] // 2
        lo_, hi_ = pl.ds(0, h), pl.ds(h, h)
        arrived(key[name, "hA", 2], region(name, 3, 0, y, core, lo_))
        arrived(key[name, "hA", 1], region(name, 3, 0, y, core, hi_))
        a = region(name, every, 0, y, core)
        key[name, "sA", 3] = send(a, a, yp)
        key[name, "sA", 1] = send(a, a, ym)
        s = region(name, pl.ds(1, 3), 0, y, core)
        key[name, "AS"] = send(s, s, sib)

    def second_ring_b(name):
        h = parts[name][2] // 2
        lo_, hi_ = pl.ds(0, h), pl.ds(h, h)
        arrived(key[name, "hB", 3], region(name, 0, 1, y2, core, lo_))
        arrived(key[name, "hB", 1], region(name, 0, 1, y2, core, hi_))
        b = region(name, 0, 1, every, core)
        key[name, "sB", 2] = send(b, region(name, 2, 1, every, core), xp)
        key[name, "sB", 1] = send(b, region(name, 1, 1, every, core), xm)
        s = region(name, 0, 1, y2, core)
        key[name, "B2S"] = send(s, s, sib)

    half_g = (pl.ds(0, GR // 2), pl.ds(GR // 2, GR // 2))

    def slot_out(s):
        a = region("g", s, 0, y, core)
        key["sA", s, 3] = send(a, a, yp)
        key["sA", s, 1] = send(a, a, ym)

    def slot_on(s):
        b3, b1 = region("g", s, 0, y3, core), region("g", s, 0, y1, core)
        arrived(key["sA", s, 3], b3)
        r = region("g", s, 0, y3, core, half_g[0])
        key["lA", s, 3] = send(r, r, yp)
        arrived(key["sA", s, 1], b1)
        r = region("g", s, 0, y1, core, half_g[1])
        key["lA", s, 1] = send(r, r, ym)
        if s == 3:
            for k, r in (("3y", region("g", 3, 0, y, core)), ("3y3", b3), ("3y1", b1)):
                key["sib", k] = send(r, r, sib)

    def slot_last(s):
        arrived(key["lA", s, 3], region("g", s, 0, y2, core, half_g[0]))
        arrived(key["lA", s, 1], region("g", s, 0, y2, core, half_g[1]))
        r = region("g", s, 0, y2 if s == 3 else every, core)
        key["sib", s] = send(r, r, sib)

    def slot_sibling(s):
        arrived(key["sib", s], region("g", s, 0, y2 if s == 3 else every, other))
        if s == 3:
            for k, yy in (("3y", y), ("3y3", y3), ("3y1", y1)):
                arrived(key["sib", k], region("g", 3, 0, yy, other))

    def second_ring_g():
        arrived(key["g", "hA", 2], region("g", 3, 0, y, core, half_g[0]))
        arrived(key["g", "hA", 1], region("g", 3, 0, y, core, half_g[1]))
        slot_out(3)
        arrived(key["g", "hB", 3], region("g", 0, 1, y2, core, half_g[0]))
        arrived(key["g", "hB", 1], region("g", 0, 1, y2, core, half_g[1]))
        b = region("g", 0, 1, every, core)
        key["g", "sB", 2] = send(b, region("g", 2, 1, every, core), xp)
        key["g", "sB", 1] = send(b, region("g", 1, 1, every, core), xm)
        s = region("g", 0, 1, y2, core)
        key["g", "B2S"] = send(s, s, sib)

    def third_g():
        b2, b1 = region("g", 2, 1, every, core), region("g", 1, 1, every, core)
        arrived(key["g", "sB", 2], b2)
        two = pl.ds(0, 2)
        key["g", "lB", 2] = send(region("g", 2, 1, two, core), region("g", 3, 1, two, core), xp)
        arrived(key["g", "sB", 1], b1)
        two = pl.ds(2, 2)
        key["g", "lB", 1] = send(region("g", 1, 1, two, core), region("g", 3, 1, two, core), xm)
        for k, s in (("tB2", b2), ("tB1", b1)):
            key["g", k] = send(s, s, sib)

    def fourth_g():
        for k, two, cc in ((2, pl.ds(0, 2), 0), (1, pl.ds(2, 2), 1)):
            s = region("g", 3, 1, two, core)
            arrived(key["g", "lB", k], s)
            key["g", "fB", k] = send(s, s, sib)

    def sibling_fourth_g():
        for k, two in ((2, pl.ds(0, 2)), (1, pl.ds(2, 2))):
            arrived(key["g", "fB", k], region("g", 3, 1, two, other))

    def third(name):
        b2, b1 = region(name, 2, 1, every, core), region(name, 1, 1, every, core)
        arrived(key[name, "sB", 2], b2)
        two = pl.ds(0, 2)
        key[name, "lB", 2] = send(region(name, 2, 1, two, core), region(name, 3, 1, two, core), xp)
        arrived(key[name, "sB", 1], b1)
        two = pl.ds(2, 2)
        key[name, "lB", 1] = send(region(name, 1, 1, two, core), region(name, 3, 1, two, core), xm)
        a3, a1 = region(name, every, 0, y3, core), region(name, every, 0, y1, core)
        arrived(key[name, "sA", 3], a3)
        s = region(name, pl.ds(0, 2), 0, y3, core)
        key[name, "lA", 3] = send(s, s, yp)
        arrived(key[name, "sA", 1], a1)
        s = region(name, pl.ds(2, 2), 0, y1, core)
        key[name, "lA", 1] = send(s, s, ym)
        for k, s in (("tB2", b2), ("tB1", b1), ("tA3", a3), ("tA1", a1)):
            key[name, k] = send(s, s, sib)

    def fourth(name):
        arrived(key[name, "lA", 3], region(name, pl.ds(0, 2), 0, y2, core))
        arrived(key[name, "lA", 1], region(name, pl.ds(2, 2), 0, y2, core))
        s = region(name, every, 0, y2, core)
        key[name, "fA"] = send(s, s, sib)
        arrived(key[name, "lB", 2], region(name, 3, 1, pl.ds(0, 2), core))
        arrived(key[name, "lB", 1], region(name, 3, 1, pl.ds(2, 2), core))
        s = region(name, 3, 1, every, core)
        key[name, "fB"] = send(s, s, sib)

    def sibling_first(name):
        arrived(key[name, "S"], region(name, 0, 1 if name == "g" else every, y, other))
        arrived(key[name, "B3S"], region(name, 0, 1, y3, other))
        arrived(key[name, "B1S"], region(name, 0, 1, y1, other))
        arrived(key[name, "B2S"], region(name, 0, 1, y2, other))

    def sibling_third(name):
        arrived(key[name, "tB2"], region(name, 2, 1, every, other))
        arrived(key[name, "tB1"], region(name, 1, 1, every, other))

    def sibling_last(name):
        arrived(key[name, "AS"], region(name, pl.ds(1, 3), 0, y, other))
        arrived(key[name, "tA3"], region(name, every, 0, y3, other))
        arrived(key[name, "tA1"], region(name, every, 0, y1, other))
        arrived(key[name, "fA"], region(name, every, 0, y2, other))
        arrived(key[name, "fB"], region(name, 3, 1, every, other))

    zeroth("g")
    zeroth("d0")
    lg = pltpu.make_async_copy(gu_hbm, wg.at[0, :, y, core], loc.at[1])
    ld = pltpu.make_async_copy(dn_hbm, wd.at[0, :, y, core], loc.at[2])
    lg.start()
    ld.start()

    lx.wait()
    xo = x_own[...]
    logits = lax.dot_general(
        router_ref[...], xo, (((1,), (1,)), ((), ())), preferred_element_type=F32
    )
    number_of = lax.broadcasted_iota(jnp.int32, (E, T), 0)
    chosen = jnp.zeros((E, T), F32)
    idx = idx_ref[0]
    for j in range(K):
        chosen = chosen + jnp.where(idx[j : j + 1, :] == number_of, 1.0, 0.0)
    sig = chosen * jax.nn.sigmoid(logits)
    gate = sig / jnp.sum(sig, axis=0, keepdims=True)
    hi = gate.astype(BF16).astype(F32)
    gall[SLOT[0]] = jnp.concatenate([hi, gate - hi], axis=0).T.astype(BF16)
    kg = {}
    kg[-1] = send(gall.at[SLOT[0]], gall.at[SLOT[-1]], zp)
    kg[1] = send(gall.at[SLOT[0]], gall.at[SLOT[1]], zm)

    def shared_expert():
        for c in shared_copies:
            c.wait()
        xo = x_own[...]
        sa = jnp.dot(xo, hid[SG : SG + D], preferred_element_type=F32)
        sb = jnp.dot(xo, hid[SU : SU + D], preferred_element_type=F32)
        sh = (jax.nn.silu(sa) * sb).astype(BF16)
        for i in range(D // FH):
            cols = slice(i * FH, (i + 1) * FH)
            shared[:, cols] = xo[:, cols].astype(F32) + jnp.dot(
                sh, hid[SD + i * FH : SD + (i + 1) * FH], preferred_element_type=F32
            )

    def token_step(d):
        for buf, keys in ((xall, kx), (gall, kg)):
            arrived(keys[-d], buf.at[SLOT[-d]])
            arrived(keys[d], buf.at[SLOT[d]])
            if d < 3:
                keys[-d - 1] = send(buf.at[SLOT[-d]], buf.at[SLOT[-d - 1]], zp)
                keys[d + 1] = send(buf.at[SLOT[d]], buf.at[SLOT[d + 1]], zm)
            else:
                lo_, hi_ = pl.ds(0, T // 2), pl.ds(T // 2, T // 2)
                keys["lo"] = send(buf.at[SLOT[-3], lo_], buf.at[SLOT[4], lo_], zp)
                keys["hi"] = send(buf.at[SLOT[3], hi_], buf.at[SLOT[4], hi_], zm)

    row_i = lax.broadcasted_iota(jnp.int32, (T, T), 0)
    col_i = lax.broadcasted_iota(jnp.int32, (T, T), 1)
    second_f = core == 1
    second_b = core == 0

    def decays():
        dtt[...] = jnp.zeros((N, T), F32)
        dtt[0:HEADS, :] = jax.nn.softplus(raw_ref[0])
        steps = dtt[...].T
        dt[...] = steps
        rate = jnp.concatenate([rate_ref[...], jnp.zeros((1, N - HEADS), F32)], axis=1)
        lower = jnp.where(row_i >= col_i, 1.0, 0.0)
        c = jnp.dot(lower, -steps * rate, precision=highest, preferred_element_type=F32)
        cum[...] = c
        cumt[...] = c.T
        b, cc = b_ref[0], c_ref[0]
        bt[...] = b.astype(F32).T.astype(BF16)
        ct[...] = cc.astype(F32).T.astype(BF16)
        lens = jnp.broadcast_to(len_ref[...].astype(F32), (8, 8))
        before = lax.broadcasted_iota(jnp.int32, (8, 8), 1) < lax.broadcasted_iota(jnp.int32, (8, 8), 0)
        starts = jnp.sum(jnp.where(before, lens, 0.0), axis=1, keepdims=True)
        offset = (ctx * T).astype(F32)
        place = lax.broadcasted_iota(jnp.int32, (8, T), 1).astype(F32) + offset

        def number(p):
            return jnp.sum(jnp.where(starts <= p, 1.0, 0.0), axis=0, keepdims=True)

        doc_row = jnp.broadcast_to(number(place), (T, T))
        doc_col = doc_row.T
        ahead = jnp.broadcast_to(number(place[:, 0:1] - 1.0), (T, T))
        final = jnp.broadcast_to(number(place[:, T - 1 : T]), (T, T))
        same[...] = jnp.where(doc_row == doc_col, 1.0, 0.0)
        end = c[T - 1 : T, :]
        carry = jnp.exp(c) * jnp.where(doc_col == ahead, 1.0, 0.0)
        close = jnp.exp(end - c) * jnp.where(doc_col == final, 1.0, 0.0) * dt[...]
        keep = jnp.exp(end) * jnp.where(final[0:1] == ahead[0:1], 1.0, 0.0)
        keeps[0] = jnp.broadcast_to(keep, (8, N))
        key["keep"] = send(keeps.at[0], keeps.at[1], sib)
        skip = jnp.concatenate([skip_ref[...], jnp.zeros((1, N - HEADS), F32)], axis=1)
        for i in range(4):
            cols = slice(i * Q, (i + 1) * Q)
            carried[:, cols] = spread_heads(carry, i * Q, Q)
            closing[:, cols] = spread_heads(close, i * Q, Q)
            skips[:, cols] = spread_heads(jnp.broadcast_to(skip, (8, N)), i * Q, Q)
            kown[:, cols] = spread_heads(keeps[0], i * Q, Q)
        aff[...] = lax.dot_general(cc, b, (((1,), (1,)), ((), ())), preferred_element_type=F32)

    def column(a, h):
        return jnp.sum(jnp.where(col_i == h, a, 0.0), axis=1, keepdims=True)

    def forward_weights():
        causal = (same[...] > 0.5) & (row_i >= col_i)
        a = aff[...]
        c = cum[...]

        def pair(p, _):
            for j in range(2):
                h = 2 * p + j
                gap = column(c, h) - cumt[pl.ds(h, 1), :]
                w = a * jnp.exp(jnp.where(causal, gap, NEG)) * dtt[pl.ds(h, 1), :]
                wmat[p, j * T : (j + 1) * T, :] = w.astype(BF16)
            return 0

        lax.fori_loop(0, HEADS // 2, pair, 0)

    def gradient_states():
        for i in range(4):
            cols = slice(i * Q, (i + 1) * Q)
            v = (carried[:, cols] * cot_ref[0, :, cols].astype(F32)).astype(BF16)
            lownb[:, cols] = jnp.dot(ct[...], v, preferred_element_type=F32).astype(BF16)
        key["lb"] = send(lownb, lsibb, sib)
        arrived(key["keep"], keeps.at[1])
        for i in range(4):
            cols = slice(i * Q, (i + 1) * Q)
            ksib[:, cols] = spread_heads(keeps[1], i * Q, Q)

    rows_own = pl.ds(pl.multiple_of(core * 64, 64), 64)
    rows_other = pl.ds(pl.multiple_of(other * 64, 64), 64)

    def chip_state(cols, lo_, ls, to, second):
        ko, ks = kown[0:1, cols], ksib[0:1, cols]
        one = jnp.ones_like(ko)
        t = jnp.where(second, one, ks) * lo_[rows_own, cols].astype(F32)
        t = t + jnp.where(second, ko, one) * ls[rows_own, cols].astype(F32)
        to[:, cols] = t.astype(BF16)

    def passed_on(cols, to, ti, so):
        k = kown[0:1, cols] * ksib[0:1, cols]
        so[:, cols] = (to[:, cols].astype(F32) + k * ti[:, cols].astype(F32)).astype(BF16)

    def entering(cols, ls, si, second):
        ks = ksib[0:1, cols]
        s = jnp.where(second, ks, jnp.ones_like(ks)) * si[:, cols].astype(F32)
        s = s + jnp.where(second, 1.0, 0.0) * ls[:, cols].astype(F32)
        return s.astype(BF16)

    def gradient_one():
        arrived(key["lb"], lsibb)
        for i in range(4):
            chip_state(slice(i * Q, (i + 1) * Q), lownb, lsibb, townb, second_b)
        key["tb"] = send(townb, tinb, ym)

    def gradient_two():
        arrived(key["tb"], tinb)
        for i in range(4):
            passed_on(slice(i * Q, (i + 1) * Q), townb, tinb, sownb)
        key["sb"] = send(sownb, sinb.at[rows_own], ym)

    def gradient_three():
        arrived(key["sb"], sinb.at[rows_own])
        key["ob"] = send(sinb.at[rows_own], sinb.at[rows_own], sib)

    def gradient_four():
        arrived(key["ob"], sinb.at[rows_other])
        causal = (same[...] > 0.5) & (row_i <= col_i)
        b = b_ref[0]
        a = lax.dot_general(b, c_ref[0], (((1,), (1,)), ((), ())), preferred_element_type=F32)
        c = cum[...]
        d = dt[...]
        left = col_i < 64

        def pair(p, _):
            cols = pl.ds(pl.multiple_of(p * N, N), N)
            seed = cot_ref[0, :, cols]
            halves = []
            for j in range(2):
                h = 2 * p + j
                gap = cumt[pl.ds(h, 1), :] - column(c, h)
                w = a * jnp.exp(jnp.where(causal, gap, NEG)) * column(d, h)
                halves.append(jnp.dot(w.astype(BF16), seed, preferred_element_type=F32))
            g = jnp.where(left, halves[0], halves[1])
            s = entering(cols, lsibb, sinb, second_b)
            g = g + closing[:, cols] * jnp.dot(b, s, preferred_element_type=F32)
            g = g + skips[0:1, cols] * seed.astype(F32)
            grad_ref[0, :, cols] = g.astype(BF16)
            return 0

        lax.fori_loop(0, HEADS // 2, pair, 0)

    def forward_zero(q, u):
        cols = slice(q * Q, (q + 1) * Q)
        v = (closing[:, cols] * u.astype(F32)).astype(BF16)
        lown[:, cols] = jnp.dot(bt[...], v, preferred_element_type=F32).astype(BF16)
        key["l", q] = send(lown.at[:, cols], lsib.at[:, cols], sib)
        left = col_i < 64
        for i in range(Q // N):
            p = q * (Q // N) + i
            pc = slice(p * N, (p + 1) * N)
            up = u[:, i * N : (i + 1) * N]
            r = jnp.dot(wmat[p], up, preferred_element_type=F32)
            intra[:, pc] = jnp.where(left, r[0:T], r[T:]) + skips[0:1, pc] * up.astype(F32)

    def forward_one(q):
        cols = slice(q * Q, (q + 1) * Q)
        arrived(key["l", q], lsib.at[:, cols])
        chip_state(cols, lown, lsib, town, second_f)
        key["t", q] = send(town.at[:, cols], tin.at[:, cols], yp)

    def forward_two(q):
        cols = slice(q * Q, (q + 1) * Q)
        arrived(key["t", q], tin.at[:, cols])
        passed_on(cols, town, tin, sown)
        key["s", q] = send(sown.at[:, cols], sin.at[rows_own, cols], yp)

    def forward_three(q):
        cols = slice(q * Q, (q + 1) * Q)
        arrived(key["s", q], sin.at[rows_own, cols])
        key["o", q] = send(sin.at[rows_own, cols], sin.at[rows_own, cols], sib)

    def forward_four(q):
        cols = slice(q * Q, (q + 1) * Q)
        arrived(key["o", q], sin.at[rows_other, cols])
        s = entering(cols, lsib, sin, second_f)
        r = intra[:, cols] + carried[:, cols] * jnp.dot(c_ref[0], s, preferred_element_type=F32)
        out_ref[0, :, cols] = r.astype(BF16)

    def hidden_tile(n, m, MT):
        slot, e = n // 2, n % 2
        away = jnp.where(slot == 2, 3, jnp.where(slot == 3, 2, slot))
        expert = 2 * (z * NX + (x + away) % NX) + e
        r = lax.broadcasted_iota(jnp.int32, (2 * E, FH), 0)
        sel = jnp.where((r == expert) | (r == expert + E), 1.0, 0.0).astype(BF16)
        xs = xall[pl.ds(m * (MT // T), MT // T)].reshape(MT, D)
        gs = gall[pl.ds(m * (MT // T), MT // T)].reshape(MT, 2 * E)
        w = wg[slot, e].reshape(D, 2 * FH)
        p = jnp.dot(xs, w, preferred_element_type=F32)
        g = jnp.dot(gs, sel, preferred_element_type=F32)
        h = (jax.nn.silu(p[:, :FH]) * p[:, FH:] * g).astype(BF16)
        hid[pl.ds(pl.multiple_of(n * NZ * T + m * MT, MT), MT), :] = h

    def hidden(experts, tiles, rows=256):
        def one(i, _):
            hidden_tile(experts[0] + experts[1] * (i // tiles[1]), tiles[0] + i % tiles[1], rows)
            return 0

        lax.fori_loop(0, experts[2] * tiles[1], one, 0)

    def partial(first, rows, hf, into):
        h = jnp.concatenate([hid[pl.ds(n * NZ * T + first * T, rows), :] for n in range(8)], axis=1)
        w = wd[:, :, :, :, :, hf * HC : (hf + 1) * HC].reshape(8 * FH, HC)
        acc = jnp.dot(h, w, preferred_element_type=F32)
        if into is part:
            part[0:rows, :] = acc
        else:
            into[:, hf * HC : (hf + 1) * HC] += acc

    kr, kl = {}, {}
    c0, c1 = slice(0, Q), slice(Q, 2 * Q)

    def scatter_start(hf):
        partial(SLOT[4], T, hf, part)
        sr[hf, 0] = part[0:T, c0].astype(BF16)
        kr[hf, 0] = send(sr.at[hf, 0], rr.at[hf, 0], zp)
        sl_[hf, 0] = part[0:T, c1].astype(BF16)
        kl[hf, 0] = send(sl_.at[hf, 0], rl.at[hf, 0], zm)
        partial(SLOT[3], 2 * T, hf, part)
        sr[hf, 1] = part[0:T, c1].astype(BF16)
        kr[hf, 1] = send(sr.at[hf, 1], rr.at[hf, 1], zp)
        sl_[hf, 1] = part[T : 2 * T, c0].astype(BF16)
        kl[hf, 1] = send(sl_.at[hf, 1], rl.at[hf, 1], zm)

    def relay(hf, k):
        cr, cl = (c0, c1) if k % 2 == 0 else (c1, c0)
        arrived(kr[hf, k], rr.at[hf, k])
        rr[hf, k] = (rr[hf, k].astype(F32) + part[0:T, cr]).astype(BF16)
        kr[hf, k + 2] = send(rr.at[hf, k], rr.at[hf, k + 2], zp)
        arrived(kl[hf, k], rl.at[hf, k])
        rl[hf, k] = (rl[hf, k].astype(F32) + part[T : 2 * T, cl]).astype(BF16)
        kl[hf, k + 2] = send(rl.at[hf, k], rl.at[hf, k + 2], zm)

    def mixer_in(hf):
        for k in (5, 6):
            arrived(kr[hf, k], rr.at[hf, k])
            arrived(kl[hf, k], rl.at[hf, k])
        for i, (a, b) in enumerate(((6, 5), (5, 6))):
            q = 2 * hf + i
            cols = slice(q * Q, (q + 1) * Q)
            u = shared[:, cols] + rr[hf, a].astype(F32) + rl[hf, b].astype(F32)
            forward_zero(q, u.astype(BF16))

    lg.wait()
    ld.wait()
    shared_expert()
    first_ring("g")
    for slot in range(3):
        slot_out(slot)
    zeroth("d1")
    decays()
    second_ring_g()
    token_step(1)
    first_ring("d0")
    slot_on(0)
    gradient_states()
    sibling_first("g")
    hidden((1, 2, 1), (3, 1))
    first_ring("d1")
    slot_on(1)
    slot_last(0)
    forward_weights()
    token_step(2)
    slot_sibling(0)
    hidden((1, 2, 1), (2, 1))
    slot_on(2)
    slot_last(1)
    hidden((0, 2, 1), (1, 1), 512)
    third_g()
    slot_sibling(1)
    hidden((2, 2, 1), (1, 1), 512)
    token_step(3)
    slot_on(3)
    second_ring_a("d0")
    slot_last(2)
    sibling_third("g")
    hidden((3, 2, 2), (1, 1), 512)
    for buf, keys in ((xall, kx), (gall, kg)):
        arrived(keys["lo"], buf.at[SLOT[4], pl.ds(0, T // 2)])
        arrived(keys["hi"], buf.at[SLOT[4], pl.ds(T // 2, T // 2)])
    slot_sibling(2)
    hidden((0, 1, 2), (0, 1), 512)
    slot_last(3)
    fourth_g()
    second_ring_b("d0")
    hidden((2, 1, 4), (0, 1), 512)
    third("d0")
    second_ring_a("d1")
    second_ring_b("d1")
    slot_sibling(3)
    sibling_fourth_g()
    hidden((4, 2, 1), (1, 1), 512)
    hidden((6, 1, 1), (0, 2), 512)
    fourth("d0")
    hidden((7, 1, 1), (0, 2), 512)
    third("d1")
    sibling_first("d0")
    sibling_third("d0")
    sibling_last("d0")
    scatter_start(0)
    relay(0, 0)
    partial(SLOT[2], 2 * T, 0, part)
    fourth("d1")
    relay(0, 1)
    relay(0, 2)
    partial(SLOT[1], 2 * T, 0, part)
    relay(0, 3)
    relay(0, 4)
    sibling_first("d1")
    sibling_third("d1")
    sibling_last("d1")
    scatter_start(1)
    partial(SLOT[0], T, 0, shared)
    mixer_in(0)
    relay(1, 0)
    partial(SLOT[2], 2 * T, 1, part)
    gradient_one()
    forward_one(0)
    forward_one(1)
    relay(1, 1)
    relay(1, 2)
    partial(SLOT[1], 2 * T, 1, part)
    gradient_two()
    forward_two(0)
    forward_two(1)
    relay(1, 3)
    relay(1, 4)
    partial(SLOT[0], T, 1, shared)
    forward_three(0)
    forward_three(1)
    gradient_three()
    gradient_four()
    forward_four(0)
    forward_four(1)
    mixer_in(1)
    for stage in (forward_one, forward_two, forward_three, forward_four):
        stage(2)
        stage(3)
    assert counter[0] == COPIES, counter
    for c in sent:
        c.wait_send()


COPIES = 2 + 2 * 27 + (5 + 6 + 16 + 4 + 3 + 3 + 4 + 2) + 2 + 12 + 28 + 1 + 4 + 16


def hand_over(a_ref, b_ref, out_a, out_b, sems):
    copies = [
        pltpu.make_async_copy(a_ref, out_a, sems.at[0]),
        pltpu.make_async_copy(b_ref, out_b, sems.at[1]),
    ]
    for c in copies:
        c.start()
    for c in copies:
        c.wait()


def on_device(
    tokens, router, gate_up, down, shared_gate_up, shared_down, routes, lengths,
    steps, writes, reads, decay_rate, skip_gain, cotangent,
):
    vmem = pl.BlockSpec(memory_space=pltpu.VMEM)
    hbm = pl.BlockSpec(memory_space=pl.ANY)
    wide = pltpu.VMEM((T, D), F32)
    square = pltpu.VMEM((T, N), F32)
    small = pltpu.VMEM((N, N), BF16)
    state = pltpu.VMEM((N, D), BF16)
    half = pltpu.VMEM((N // 2, D), BF16)
    row = pltpu.VMEM((8, D), F32)
    out, grad = pl.pallas_call(
        kernel,
        out_shape=[jax.ShapeDtypeStruct((1, T, D), BF16)] * 2,
        in_specs=[hbm, vmem, hbm, hbm, hbm, hbm] + [vmem] * 8,
        out_specs=[vmem, vmem],
        scratch_shapes=[
            pltpu.VMEM((NZ, T, D), BF16),
            pltpu.VMEM((NZ, T, 2 * E), BF16),
            pltpu.VMEM((NX, 2, NY, 2, GR, 2 * FH), BF16),
            pltpu.VMEM((NX, 2, NY, 2, DR, D), BF16),
            pltpu.VMEM((NX * 2 * NZ * T, FH), BF16),
            pltpu.VMEM((2 * T, 2 * Q), F32),
            wide,
            pltpu.VMEM((2, 7, T, Q), BF16),
            pltpu.VMEM((2, 7, T, Q), BF16),
            pltpu.VMEM((2, 2, T, Q), BF16),
            pltpu.VMEM((2, 2, T, Q), BF16),
            square, square, square, square, square, square, small, small, wide, wide,
            pltpu.VMEM((HEADS // 2, 2 * T, T), BF16),
            pltpu.VMEM((2, 8, N), F32),
            row, row, row, wide,
            state, state, half, half, half, state,
            state, state, half, half, half, state,
            pltpu.SemaphoreType.DMA((5 + D // FH,)),
            pltpu.SemaphoreType.DMA((COPIES,)),
            pltpu.SemaphoreType.DMA((COPIES,)),
        ],
        compiler_params=pltpu.CompilerParams(
            collective_id=0, has_side_effects=True, vmem_limit_bytes=63 * 2**20
        ),
    )(
        tokens, router.T, gate_up, down, shared_gate_up, shared_down, jnp.swapaxes(routes, 1, 2), lengths,
        jnp.swapaxes(steps, 1, 2), writes, reads, decay_rate.reshape(1, -1), skip_gain.reshape(1, -1), cotangent,
    )
    return pl.pallas_call(
        hand_over,
        out_shape=[jax.ShapeDtypeStruct((1, T, D), BF16)] * 2,
        in_specs=[hbm, hbm],
        out_specs=[hbm, hbm],
        scratch_shapes=[pltpu.SemaphoreType.DMA((2,))],
    )(out, grad)


def solution(mesh):
    return jax.shard_map(
        on_device,
        mesh=mesh,
        in_specs=(
            P("exp", "ctx", None),
            P(),
            P("exp", "ctx", None),
            P("exp", "ctx", None),
            P(),
            P(),
            P("exp", "ctx", None),
            P("exp", None),
            P("exp", "ctx", None),
            P("exp", "ctx", None),
            P("exp", "ctx", None),
            P(),
            P(),
            P("exp", "ctx", None),
        ),
        out_specs=(P("exp", "ctx", None), P("exp", "ctx", None)),
        check_vma=False,
    )
```

```python
import functools

import jax
import jax.numpy as jnp
from jax import lax
from jax.experimental import pallas as pl
from jax.experimental.pallas import tpu as pltpu
from jax.sharding import PartitionSpec as P

highest = lax.Precision.HIGHEST
MESH = pl.DeviceIdType.MESH
F32 = jnp.float32
BF16 = jnp.bfloat16

T = 128
D = 2560
E = 64
K = 8
FH = 256
NZ, NX, NY = 8, 4, 4
GR = D // 8
DR = FH // 8
HEADS = 40
N = 128
Q = D // 4
NEG = -1e30
SLOT = {4: 0, 3: 1, -3: 2, 2: 3, -2: 4, 1: 5, -1: 6, 0: 7}


def head_columns(first, count):
    h = lax.broadcasted_iota(jnp.int32, (N, count), 0)
    c = lax.broadcasted_iota(jnp.int32, (N, count), 1) + first
    return jnp.where((c >= h * 64) & (c < h * 64 + 64), 1.0, 0.0).astype(BF16)


def spread_heads(a, first, count):
    pick = head_columns(first, count)
    hi = a.astype(BF16)
    lo = (a - hi.astype(F32)).astype(BF16)
    return jnp.dot(hi, pick, preferred_element_type=F32) + jnp.dot(lo, pick, preferred_element_type=F32)


def kernel(
    x_hbm, router_ref, gu_hbm, dn_hbm, sgu_hbm, sdn_hbm, idx_ref, len_ref, raw_ref, b_ref, c_ref,
    rate_ref, skip_ref, cot_ref, out_ref, grad_ref,
    xall, gall, wg, wd, hid, part, shared, rr, rl, sr, sl_,
    cum, cumt, dt, dtt, aff, same, bt, ct, carried, closing, wmat, keeps, kown, ksib, skips, intra,
    lown, lsib, town, tin, sown, sin, lownb, lsibb, townb, tinb, sownb, sinb,
    loc, ss, rs,
):
    ctx = lax.axis_index("ctx")
    exp = lax.axis_index("exp")
    z, x = exp // NX, exp % NX
    y, core = ctx // 2, ctx % 2
    zp = {"exp": (exp + NX) % (NX * NZ)}
    zm = {"exp": (exp + NX * (NZ - 1)) % (NX * NZ)}
    xp = {"exp": z * NX + (x + 1) % NX}
    xm = {"exp": z * NX + (x + NX - 1) % NX}
    yp = {"ctx": (ctx + 2) % 8}
    ym = {"ctx": (ctx + 6) % 8}
    sib = {"ctx": ctx + 1 - 2 * core}
    y1, y2, y3 = (y + 1) % NY, (y + 2) % NY, (y + 3) % NY
    other = 1 - core

    counter = [0]

    def rcopy(src, dst, dev, k):
        return pltpu.make_async_remote_copy(
            src_ref=src, dst_ref=dst, send_sem=ss.at[k], recv_sem=rs.at[k],
            device_id=dev, device_id_type=MESH,
        )

    sent = []

    def send(src, dst, dev):
        k = counter[0]
        counter[0] += 1
        c = rcopy(src, dst, dev, k)
        c.start()
        sent.append(c)
        return k

    def arrived(k, region):
        rcopy(region, region, sib, k).wait_recv()

    barrier = pltpu.get_barrier_semaphore()
    for dev in (zp, zm, xp, xm, yp, ym, sib):
        pl.semaphore_signal(barrier, inc=1, device_id=dev, device_id_type=MESH)

    x_own = xall.at[SLOT[0]]
    lx = pltpu.make_async_copy(x_hbm.at[0], x_own, loc.at[0])
    lx.start()
    SG, SU, SD = 0, D, 2 * D
    shared_copies = [
        pltpu.make_async_copy(sgu_hbm.at[:, pl.ds(0, FH)], hid.at[pl.ds(SG, D)], loc.at[3]),
        pltpu.make_async_copy(sgu_hbm.at[:, pl.ds(FH, FH)], hid.at[pl.ds(SU, D)], loc.at[4]),
    ] + [
        pltpu.make_async_copy(
            sdn_hbm.at[:, pl.ds(i * FH, FH)], hid.at[pl.ds(SD + i * FH, FH)], loc.at[5 + i]
        )
        for i in range(D // FH)
    ]
    for c in shared_copies:
        c.start()
    pl.semaphore_wait(barrier, 7)

    kx = {}
    kx[-1] = send(x_hbm.at[0], xall.at[SLOT[-1]], zp)
    kx[1] = send(x_hbm.at[0], xall.at[SLOT[1]], zm)

    HC = D // 2
    parts = {"g": (gu_hbm, wg, GR, None), "d0": (dn_hbm, wd, DR, pl.ds(0, HC)), "d1": (dn_hbm, wd, DR, pl.ds(HC, HC))}

    def region(name, slot, e, yy, cc, rows=slice(None)):
        w, cols = parts[name][1], parts[name][3]
        return w.at[slot, e, yy, cc, rows] if cols is None else w.at[slot, e, yy, cc, rows, cols]

    def mine(name, e):
        w, cols = parts[name][0], parts[name][3]
        if e is None:
            return w if cols is None else w.at[:, :, cols]
        return w.at[e] if cols is None else w.at[e, :, cols]

    key = {}
    every = slice(None)

    def zeroth(name):
        key[name, "A", 2] = send(mine(name, 0), region(name, 2, 0, y, core), xp)
        key[name, "A", 1] = send(mine(name, 0), region(name, 1, 0, y, core), xm)
        key[name, "B", 3] = send(mine(name, 1), region(name, 0, 1, y, core), yp)
        key[name, "B", 1] = send(mine(name, 1), region(name, 0, 1, y, core), ym)
        own = 1 if name == "g" else None
        key[name, "S"] = send(mine(name, own), region(name, 0, every if own is None else own, y, core), sib)

    def first_ring(name):
        h = parts[name][2] // 2
        lo_, hi_ = pl.ds(0, h), pl.ds(h, h)
        arrived(key[name, "A", 2], region(name, 2, 0, y, core))
        key[name, "hA", 2] = send(region(name, 2, 0, y, core, lo_), region(name, 3, 0, y, core, lo_), xp)
        arrived(key[name, "A", 1], region(name, 1, 0, y, core))
        key[name, "hA", 1] = send(region(name, 1, 0, y, core, hi_), region(name, 3, 0, y, core, hi_), xm)
        b3, b1 = region(name, 0, 1, y3, core), region(name, 0, 1, y1, core)
        arrived(key[name, "B", 3], b3)
        key[name, "hB", 3] = send(region(name, 0, 1, y3, core, lo_), region(name, 0, 1, y3, core, lo_), yp)
        arrived(key[name, "B", 1], b1)
        key[name, "hB", 1] = send(region(name, 0, 1, y1, core, hi_), region(name, 0, 1, y1, core, hi_), ym)
        key[name, "B3S"] = send(b3, b3, sib)
        key[name, "B1S"] = send(b1, b1, sib)

    def second_ring_a(name):
        h = parts[name][2] // 2
        lo_, hi_ = pl.ds(0, h), pl.ds(h, h)
        arrived(key[name, "hA", 2], region(name, 3, 0, y, core, lo_))
        arrived(key[name, "hA", 1], region(name, 3, 0, y, core, hi_))
        a = region(name, every, 0, y, core)
        key[name, "sA", 3] = send(a, a, yp)
        key[name, "sA", 1] = send(a, a, ym)
        s = region(name, pl.ds(1, 3), 0, y, core)
        key[name, "AS"] = send(s, s, sib)

    def second_ring_b(name):
        h = parts[name][2] // 2
        lo_, hi_ = pl.ds(0, h), pl.ds(h, h)
        arrived(key[name, "hB", 3], region(name, 0, 1, y2, core, lo_))
        arrived(key[name, "hB", 1], region(name, 0, 1, y2, core, hi_))
        b = region(name, 0, 1, every, core)
        key[name, "sB", 2] = send(b, region(name, 2, 1, every, core), xp)
        key[name, "sB", 1] = send(b, region(name, 1, 1, every, core), xm)
        s = region(name, 0, 1, y2, core)
        key[name, "B2S"] = send(s, s, sib)

    half_g = (pl.ds(0, GR // 2), pl.ds(GR // 2, GR // 2))

    def slot_out(s):
        a = region("g", s, 0, y, core)
        key["sA", s, 3] = send(a, a, yp)
        key["sA", s, 1] = send(a, a, ym)

    def slot_on(s):
        b3, b1 = region("g", s, 0, y3, core), region("g", s, 0, y1, core)
        arrived(key["sA", s, 3], b3)
        r = region("g", s, 0, y3, core, half_g[0])
        key["lA", s, 3] = send(r, r, yp)
        arrived(key["sA", s, 1], b1)
        r = region("g", s, 0, y1, core, half_g[1])
        key["lA", s, 1] = send(r, r, ym)
        if s == 3:
            for k, r in (("3y", region("g", 3, 0, y, core)), ("3y3", b3), ("3y1", b1)):
                key["sib", k] = send(r, r, sib)

    def slot_last(s):
        arrived(key["lA", s, 3], region("g", s, 0, y2, core, half_g[0]))
        arrived(key["lA", s, 1], region("g", s, 0, y2, core, half_g[1]))
        r = region("g", s, 0, y2 if s == 3 else every, core)
        key["sib", s] = send(r, r, sib)

    def slot_sibling(s):
        arrived(key["sib", s], region("g", s, 0, y2 if s == 3 else every, other))
        if s == 3:
            for k, yy in (("3y", y), ("3y3", y3), ("3y1", y1)):
                arrived(key["sib", k], region("g", 3, 0, yy, other))

    def second_ring_g():
        arrived(key["g", "hA", 2], region("g", 3, 0, y, core, half_g[0]))
        arrived(key["g", "hA", 1], region("g", 3, 0, y, core, half_g[1]))
        slot_out(3)
        arrived(key["g", "hB", 3], region("g", 0, 1, y2, core, half_g[0]))
        arrived(key["g", "hB", 1], region("g", 0, 1, y2, core, half_g[1]))
        b = region("g", 0, 1, every, core)
        key["g", "sB", 2] = send(b, region("g", 2, 1, every, core), xp)
        key["g", "sB", 1] = send(b, region("g", 1, 1, every, core), xm)
        s = region("g", 0, 1, y2, core)
        key["g", "B2S"] = send(s, s, sib)

    def third_g():
        b2, b1 = region("g", 2, 1, every, core), region("g", 1, 1, every, core)
        arrived(key["g", "sB", 2], b2)
        two = pl.ds(0, 2)
        key["g", "lB", 2] = send(region("g", 2, 1, two, core), region("g", 3, 1, two, core), xp)
        arrived(key["g", "sB", 1], b1)
        two = pl.ds(2, 2)
        key["g", "lB", 1] = send(region("g", 1, 1, two, core), region("g", 3, 1, two, core), xm)
        for k, s in (("tB2", b2), ("tB1", b1)):
            key["g", k] = send(s, s, sib)

    def fourth_g():
        for k, two, cc in ((2, pl.ds(0, 2), 0), (1, pl.ds(2, 2), 1)):
            s = region("g", 3, 1, two, core)
            arrived(key["g", "lB", k], s)
            key["g", "fB", k] = send(s, s, sib)

    def sibling_fourth_g():
        for k, two in ((2, pl.ds(0, 2)), (1, pl.ds(2, 2))):
            arrived(key["g", "fB", k], region("g", 3, 1, two, other))

    def third(name):
        b2, b1 = region(name, 2, 1, every, core), region(name, 1, 1, every, core)
        arrived(key[name, "sB", 2], b2)
        two = pl.ds(0, 2)
        key[name, "lB", 2] = send(region(name, 2, 1, two, core), region(name, 3, 1, two, core), xp)
        arrived(key[name, "sB", 1], b1)
        two = pl.ds(2, 2)
        key[name, "lB", 1] = send(region(name, 1, 1, two, core), region(name, 3, 1, two, core), xm)
        a3, a1 = region(name, every, 0, y3, core), region(name, every, 0, y1, core)
        arrived(key[name, "sA", 3], a3)
        s = region(name, pl.ds(0, 2), 0, y3, core)
        key[name, "lA", 3] = send(s, s, yp)
        arrived(key[name, "sA", 1], a1)
        s = region(name, pl.ds(2, 2), 0, y1, core)
        key[name, "lA", 1] = send(s, s, ym)
        for k, s in (("tB2", b2), ("tB1", b1), ("tA3", a3), ("tA1", a1)):
            key[name, k] = send(s, s, sib)

    def fourth(name):
        arrived(key[name, "lA", 3], region(name, pl.ds(0, 2), 0, y2, core))
        arrived(key[name, "lA", 1], region(name, pl.ds(2, 2), 0, y2, core))
        s = region(name, every, 0, y2, core)
        key[name, "fA"] = send(s, s, sib)
        arrived(key[name, "lB", 2], region(name, 3, 1, pl.ds(0, 2), core))
        arrived(key[name, "lB", 1], region(name, 3, 1, pl.ds(2, 2), core))
        s = region(name, 3, 1, every, core)
        key[name, "fB"] = send(s, s, sib)

    def sibling_first(name):
        arrived(key[name, "S"], region(name, 0, 1 if name == "g" else every, y, other))
        arrived(key[name, "B3S"], region(name, 0, 1, y3, other))
        arrived(key[name, "B1S"], region(name, 0, 1, y1, other))
        arrived(key[name, "B2S"], region(name, 0, 1, y2, other))

    def sibling_third(name):
        arrived(key[name, "tB2"], region(name, 2, 1, every, other))
        arrived(key[name, "tB1"], region(name, 1, 1, every, other))

    def sibling_last(name):
        arrived(key[name, "AS"], region(name, pl.ds(1, 3), 0, y, other))
        arrived(key[name, "tA3"], region(name, every, 0, y3, other))
        arrived(key[name, "tA1"], region(name, every, 0, y1, other))
        arrived(key[name, "fA"], region(name, every, 0, y2, other))
        arrived(key[name, "fB"], region(name, 3, 1, every, other))

    for name in ("g", "d0", "d1"):
        zeroth(name)
    lg = pltpu.make_async_copy(gu_hbm, wg.at[0, :, y, core], loc.at[1])
    ld = pltpu.make_async_copy(dn_hbm, wd.at[0, :, y, core], loc.at[2])
    lg.start()
    ld.start()

    lx.wait()
    xo = x_own[...]
    logits = lax.dot_general(
        router_ref[...], xo, (((1,), (1,)), ((), ())), preferred_element_type=F32
    )
    number_of = lax.broadcasted_iota(jnp.int32, (E, T), 0)
    chosen = jnp.zeros((E, T), F32)
    idx = idx_ref[0]
    for j in range(K):
        chosen = chosen + jnp.where(idx[j : j + 1, :] == number_of, 1.0, 0.0)
    sig = chosen * jax.nn.sigmoid(logits)
    gate = sig / jnp.sum(sig, axis=0, keepdims=True)
    hi = gate.astype(BF16).astype(F32)
    gall[SLOT[0]] = jnp.concatenate([hi, gate - hi], axis=0).T.astype(BF16)
    kg = {}
    kg[-1] = send(gall.at[SLOT[0]], gall.at[SLOT[-1]], zp)
    kg[1] = send(gall.at[SLOT[0]], gall.at[SLOT[1]], zm)

    def shared_expert():
        for c in shared_copies:
            c.wait()
        xo = x_own[...]
        sa = jnp.dot(xo, hid[SG : SG + D], preferred_element_type=F32)
        sb = jnp.dot(xo, hid[SU : SU + D], preferred_element_type=F32)
        sh = (jax.nn.silu(sa) * sb).astype(BF16)
        for i in range(D // FH):
            cols = slice(i * FH, (i + 1) * FH)
            shared[:, cols] = xo[:, cols].astype(F32) + jnp.dot(
                sh, hid[SD + i * FH : SD + (i + 1) * FH], preferred_element_type=F32
            )

    def token_step(d):
        for buf, keys in ((xall, kx), (gall, kg)):
            arrived(keys[-d], buf.at[SLOT[-d]])
            arrived(keys[d], buf.at[SLOT[d]])
            if d < 3:
                keys[-d - 1] = send(buf.at[SLOT[-d]], buf.at[SLOT[-d - 1]], zp)
                keys[d + 1] = send(buf.at[SLOT[d]], buf.at[SLOT[d + 1]], zm)
            else:
                lo_, hi_ = pl.ds(0, T // 2), pl.ds(T // 2, T // 2)
                keys["lo"] = send(buf.at[SLOT[-3], lo_], buf.at[SLOT[4], lo_], zp)
                keys["hi"] = send(buf.at[SLOT[3], hi_], buf.at[SLOT[4], hi_], zm)

    row_i = lax.broadcasted_iota(jnp.int32, (T, T), 0)
    col_i = lax.broadcasted_iota(jnp.int32, (T, T), 1)
    second_f = core == 1
    second_b = core == 0

    def decays():
        dtt[...] = jnp.zeros((N, T), F32)
        dtt[0:HEADS, :] = jax.nn.softplus(raw_ref[0])
        steps = dtt[...].T
        dt[...] = steps
        rate = jnp.concatenate([rate_ref[...], jnp.zeros((1, N - HEADS), F32)], axis=1)
        lower = jnp.where(row_i >= col_i, 1.0, 0.0)
        c = jnp.dot(lower, -steps * rate, precision=highest, preferred_element_type=F32)
        cum[...] = c
        cumt[...] = c.T
        b, cc = b_ref[0], c_ref[0]
        bt[...] = b.astype(F32).T.astype(BF16)
        ct[...] = cc.astype(F32).T.astype(BF16)
        lens = jnp.broadcast_to(len_ref[...].astype(F32), (8, 8))
        before = lax.broadcasted_iota(jnp.int32, (8, 8), 1) < lax.broadcasted_iota(jnp.int32, (8, 8), 0)
        starts = jnp.sum(jnp.where(before, lens, 0.0), axis=1, keepdims=True)
        offset = (ctx * T).astype(F32)
        place = lax.broadcasted_iota(jnp.int32, (8, T), 1).astype(F32) + offset

        def number(p):
            return jnp.sum(jnp.where(starts <= p, 1.0, 0.0), axis=0, keepdims=True)

        doc_row = jnp.broadcast_to(number(place), (T, T))
        doc_col = doc_row.T
        ahead = jnp.broadcast_to(number(place[:, 0:1] - 1.0), (T, T))
        final = jnp.broadcast_to(number(place[:, T - 1 : T]), (T, T))
        same[...] = jnp.where(doc_row == doc_col, 1.0, 0.0)
        end = c[T - 1 : T, :]
        carry = jnp.exp(c) * jnp.where(doc_col == ahead, 1.0, 0.0)
        close = jnp.exp(end - c) * jnp.where(doc_col == final, 1.0, 0.0) * dt[...]
        keep = jnp.exp(end) * jnp.where(final[0:1] == ahead[0:1], 1.0, 0.0)
        keeps[0] = jnp.broadcast_to(keep, (8, N))
        key["keep"] = send(keeps.at[0], keeps.at[1], sib)
        skip = jnp.concatenate([skip_ref[...], jnp.zeros((1, N - HEADS), F32)], axis=1)
        for i in range(4):
            cols = slice(i * Q, (i + 1) * Q)
            carried[:, cols] = spread_heads(carry, i * Q, Q)
            closing[:, cols] = spread_heads(close, i * Q, Q)
            skips[:, cols] = spread_heads(jnp.broadcast_to(skip, (8, N)), i * Q, Q)
            kown[:, cols] = spread_heads(keeps[0], i * Q, Q)
        aff[...] = lax.dot_general(cc, b, (((1,), (1,)), ((), ())), preferred_element_type=F32)

    def column(a, h):
        return jnp.sum(jnp.where(col_i == h, a, 0.0), axis=1, keepdims=True)

    def forward_weights():
        causal = (same[...] > 0.5) & (row_i >= col_i)
        a = aff[...]
        c = cum[...]

        def pair(p, _):
            for j in range(2):
                h = 2 * p + j
                gap = column(c, h) - cumt[pl.ds(h, 1), :]
                w = a * jnp.exp(jnp.where(causal, gap, NEG)) * dtt[pl.ds(h, 1), :]
                wmat[p, j * T : (j + 1) * T, :] = w.astype(BF16)
            return 0

        lax.fori_loop(0, HEADS // 2, pair, 0)

    def gradient_states():
        for i in range(4):
            cols = slice(i * Q, (i + 1) * Q)
            v = (carried[:, cols] * cot_ref[0, :, cols].astype(F32)).astype(BF16)
            lownb[:, cols] = jnp.dot(ct[...], v, preferred_element_type=F32).astype(BF16)
        key["lb"] = send(lownb, lsibb, sib)
        arrived(key["keep"], keeps.at[1])
        for i in range(4):
            cols = slice(i * Q, (i + 1) * Q)
            ksib[:, cols] = spread_heads(keeps[1], i * Q, Q)

    rows_own = pl.ds(pl.multiple_of(core * 64, 64), 64)
    rows_other = pl.ds(pl.multiple_of(other * 64, 64), 64)

    def chip_state(cols, lo_, ls, to, second):
        ko, ks = kown[0:1, cols], ksib[0:1, cols]
        one = jnp.ones_like(ko)
        t = jnp.where(second, one, ks) * lo_[rows_own, cols].astype(F32)
        t = t + jnp.where(second, ko, one) * ls[rows_own, cols].astype(F32)
        to[:, cols] = t.astype(BF16)

    def passed_on(cols, to, ti, so):
        k = kown[0:1, cols] * ksib[0:1, cols]
        so[:, cols] = (to[:, cols].astype(F32) + k * ti[:, cols].astype(F32)).astype(BF16)

    def entering(cols, ls, si, second):
        ks = ksib[0:1, cols]
        s = jnp.where(second, ks, jnp.ones_like(ks)) * si[:, cols].astype(F32)
        s = s + jnp.where(second, 1.0, 0.0) * ls[:, cols].astype(F32)
        return s.astype(BF16)

    def gradient_one():
        arrived(key["lb"], lsibb)
        for i in range(4):
            chip_state(slice(i * Q, (i + 1) * Q), lownb, lsibb, townb, second_b)
        key["tb"] = send(townb, tinb, ym)

    def gradient_two():
        arrived(key["tb"], tinb)
        for i in range(4):
            passed_on(slice(i * Q, (i + 1) * Q), townb, tinb, sownb)
        key["sb"] = send(sownb, sinb.at[rows_own], ym)

    def gradient_three():
        arrived(key["sb"], sinb.at[rows_own])
        key["ob"] = send(sinb.at[rows_own], sinb.at[rows_own], sib)

    def gradient_four():
        arrived(key["ob"], sinb.at[rows_other])
        causal = (same[...] > 0.5) & (row_i <= col_i)
        b = b_ref[0]
        a = lax.dot_general(b, c_ref[0], (((1,), (1,)), ((), ())), preferred_element_type=F32)
        c = cum[...]
        d = dt[...]
        left = col_i < 64

        def pair(p, _):
            cols = pl.ds(pl.multiple_of(p * N, N), N)
            seed = cot_ref[0, :, cols]
            halves = []
            for j in range(2):
                h = 2 * p + j
                gap = cumt[pl.ds(h, 1), :] - column(c, h)
                w = a * jnp.exp(jnp.where(causal, gap, NEG)) * column(d, h)
                halves.append(jnp.dot(w.astype(BF16), seed, preferred_element_type=F32))
            g = jnp.where(left, halves[0], halves[1])
            s = entering(cols, lsibb, sinb, second_b)
            g = g + closing[:, cols] * jnp.dot(b, s, preferred_element_type=F32)
            g = g + skips[0:1, cols] * seed.astype(F32)
            grad_ref[0, :, cols] = g.astype(BF16)
            return 0

        lax.fori_loop(0, HEADS // 2, pair, 0)

    def forward_zero(q, u):
        cols = slice(q * Q, (q + 1) * Q)
        v = (closing[:, cols] * u.astype(F32)).astype(BF16)
        lown[:, cols] = jnp.dot(bt[...], v, preferred_element_type=F32).astype(BF16)
        key["l", q] = send(lown.at[:, cols], lsib.at[:, cols], sib)
        left = col_i < 64
        for i in range(Q // N):
            p = q * (Q // N) + i
            pc = slice(p * N, (p + 1) * N)
            up = u[:, i * N : (i + 1) * N]
            r = jnp.dot(wmat[p], up, preferred_element_type=F32)
            intra[:, pc] = jnp.where(left, r[0:T], r[T:]) + skips[0:1, pc] * up.astype(F32)

    def forward_one(q):
        cols = slice(q * Q, (q + 1) * Q)
        arrived(key["l", q], lsib.at[:, cols])
        chip_state(cols, lown, lsib, town, second_f)
        key["t", q] = send(town.at[:, cols], tin.at[:, cols], yp)

    def forward_two(q):
        cols = slice(q * Q, (q + 1) * Q)
        arrived(key["t", q], tin.at[:, cols])
        passed_on(cols, town, tin, sown)
        key["s", q] = send(sown.at[:, cols], sin.at[rows_own, cols], yp)

    def forward_three(q):
        cols = slice(q * Q, (q + 1) * Q)
        arrived(key["s", q], sin.at[rows_own, cols])
        key["o", q] = send(sin.at[rows_own, cols], sin.at[rows_own, cols], sib)

    def forward_four(q):
        cols = slice(q * Q, (q + 1) * Q)
        arrived(key["o", q], sin.at[rows_other, cols])
        s = entering(cols, lsib, sin, second_f)
        r = intra[:, cols] + carried[:, cols] * jnp.dot(c_ref[0], s, preferred_element_type=F32)
        out_ref[0, :, cols] = r.astype(BF16)

    def hidden_tile(n, m, MT):
        slot, e = n // 2, n % 2
        away = jnp.where(slot == 2, 3, jnp.where(slot == 3, 2, slot))
        expert = 2 * (z * NX + (x + away) % NX) + e
        r = lax.broadcasted_iota(jnp.int32, (2 * E, FH), 0)
        sel = jnp.where((r == expert) | (r == expert + E), 1.0, 0.0).astype(BF16)
        xs = xall[pl.ds(m * (MT // T), MT // T)].reshape(MT, D)
        gs = gall[pl.ds(m * (MT // T), MT // T)].reshape(MT, 2 * E)
        w = wg[slot, e].reshape(D, 2 * FH)
        p = jnp.dot(xs, w, preferred_element_type=F32)
        g = jnp.dot(gs, sel, preferred_element_type=F32)
        h = (jax.nn.silu(p[:, :FH]) * p[:, FH:] * g).astype(BF16)
        hid[pl.ds(pl.multiple_of(n * NZ * T + m * MT, MT), MT), :] = h

    def hidden(experts, tiles, rows=256):
        def one(i, _):
            hidden_tile(experts[0] + experts[1] * (i // tiles[1]), tiles[0] + i % tiles[1], rows)
            return 0

        lax.fori_loop(0, experts[2] * tiles[1], one, 0)

    def partial(first, rows, hf, into):
        h = jnp.concatenate([hid[pl.ds(n * NZ * T + first * T, rows), :] for n in range(8)], axis=1)
        w = wd[:, :, :, :, :, hf * HC : (hf + 1) * HC].reshape(8 * FH, HC)
        acc = jnp.dot(h, w, preferred_element_type=F32)
        if into is part:
            part[0:rows, :] = acc
        else:
            into[:, hf * HC : (hf + 1) * HC] += acc

    kr, kl = {}, {}
    c0, c1 = slice(0, Q), slice(Q, 2 * Q)

    def scatter_start(hf):
        partial(SLOT[4], T, hf, part)
        sr[hf, 0] = part[0:T, c0].astype(BF16)
        kr[hf, 0] = send(sr.at[hf, 0], rr.at[hf, 0], zp)
        sl_[hf, 0] = part[0:T, c1].astype(BF16)
        kl[hf, 0] = send(sl_.at[hf, 0], rl.at[hf, 0], zm)
        partial(SLOT[3], 2 * T, hf, part)
        sr[hf, 1] = part[0:T, c1].astype(BF16)
        kr[hf, 1] = send(sr.at[hf, 1], rr.at[hf, 1], zp)
        sl_[hf, 1] = part[T : 2 * T, c0].astype(BF16)
        kl[hf, 1] = send(sl_.at[hf, 1], rl.at[hf, 1], zm)

    def relay(hf, k):
        cr, cl = (c0, c1) if k % 2 == 0 else (c1, c0)
        arrived(kr[hf, k], rr.at[hf, k])
        rr[hf, k] = (rr[hf, k].astype(F32) + part[0:T, cr]).astype(BF16)
        kr[hf, k + 2] = send(rr.at[hf, k], rr.at[hf, k + 2], zp)
        arrived(kl[hf, k], rl.at[hf, k])
        rl[hf, k] = (rl[hf, k].astype(F32) + part[T : 2 * T, cl]).astype(BF16)
        kl[hf, k + 2] = send(rl.at[hf, k], rl.at[hf, k + 2], zm)

    def mixer_in(hf):
        for k in (5, 6):
            arrived(kr[hf, k], rr.at[hf, k])
            arrived(kl[hf, k], rl.at[hf, k])
        for i, (a, b) in enumerate(((6, 5), (5, 6))):
            q = 2 * hf + i
            cols = slice(q * Q, (q + 1) * Q)
            u = shared[:, cols] + rr[hf, a].astype(F32) + rl[hf, b].astype(F32)
            forward_zero(q, u.astype(BF16))

    lg.wait()
    ld.wait()
    shared_expert()
    decays()
    first_ring("g")
    for slot in range(3):
        slot_out(slot)
    first_ring("d0")
    first_ring("d1")
    token_step(1)
    second_ring_g()
    gradient_states()
    forward_weights()
    sibling_first("g")
    hidden((1, 2, 1), (3, 1))
    slot_on(0)
    slot_on(1)
    token_step(2)
    hidden((1, 2, 1), (2, 1))
    slot_on(2)
    token_step(3)
    slot_on(3)
    third_g()
    second_ring_a("d0")
    second_ring_b("d0")
    slot_last(0)
    sibling_third("g")
    hidden((3, 2, 2), (1, 1), 512)
    slot_last(1)
    slot_sibling(0)
    hidden((0, 1, 1), (1, 1), 512)
    for buf, keys in ((xall, kx), (gall, kg)):
        arrived(keys["lo"], buf.at[SLOT[4], pl.ds(0, T // 2)])
        arrived(keys["hi"], buf.at[SLOT[4], pl.ds(T // 2, T // 2)])
    slot_last(2)
    hidden((1, 2, 2), (0, 1), 512)
    slot_sibling(1)
    hidden((2, 1, 1), (1, 1), 512)
    slot_last(3)
    fourth_g()
    hidden((5, 1, 1), (0, 1), 512)
    hidden((0, 2, 2), (0, 1), 512)
    slot_sibling(2)
    hidden((4, 1, 1), (0, 2), 512)
    third("d0")
    second_ring_a("d1")
    second_ring_b("d1")
    slot_sibling(3)
    hidden((6, 1, 1), (0, 2), 512)
    fourth("d0")
    sibling_fourth_g()
    hidden((7, 1, 1), (0, 2), 512)
    sibling_first("d0")
    sibling_third("d0")
    sibling_last("d0")
    scatter_start(0)
    third("d1")
    relay(0, 0)
    partial(SLOT[2], 2 * T, 0, part)
    fourth("d1")
    relay(0, 1)
    relay(0, 2)
    partial(SLOT[1], 2 * T, 0, part)
    relay(0, 3)
    relay(0, 4)
    sibling_first("d1")
    sibling_third("d1")
    sibling_last("d1")
    scatter_start(1)
    partial(SLOT[0], T, 0, shared)
    mixer_in(0)
    relay(1, 0)
    partial(SLOT[2], 2 * T, 1, part)
    gradient_one()
    forward_one(0)
    forward_one(1)
    relay(1, 1)
    relay(1, 2)
    partial(SLOT[1], 2 * T, 1, part)
    gradient_two()
    forward_two(0)
    forward_two(1)
    relay(1, 3)
    relay(1, 4)
    partial(SLOT[0], T, 1, shared)
    forward_three(0)
    forward_three(1)
    gradient_three()
    gradient_four()
    forward_four(0)
    forward_four(1)
    mixer_in(1)
    for stage in (forward_one, forward_two, forward_three, forward_four):
        stage(2)
        stage(3)
    assert counter[0] == COPIES, counter
    for c in sent:
        c.wait_send()


COPIES = 2 + 2 * 27 + (5 + 6 + 16 + 4 + 3 + 3 + 4 + 2) + 2 + 12 + 28 + 1 + 4 + 16


def hand_over(a_ref, b_ref, out_a, out_b):
    out_a[...] = a_ref[...]
    out_b[...] = b_ref[...]


def on_device(
    tokens, router, gate_up, down, shared_gate_up, shared_down, routes, lengths,
    steps, writes, reads, decay_rate, skip_gain, cotangent,
):
    vmem = pl.BlockSpec(memory_space=pltpu.VMEM)
    hbm = pl.BlockSpec(memory_space=pl.ANY)
    wide = pltpu.VMEM((T, D), F32)
    square = pltpu.VMEM((T, N), F32)
    small = pltpu.VMEM((N, N), BF16)
    state = pltpu.VMEM((N, D), BF16)
    half = pltpu.VMEM((N // 2, D), BF16)
    row = pltpu.VMEM((8, D), F32)
    out, grad = pl.pallas_call(
        kernel,
        out_shape=[jax.ShapeDtypeStruct((1, T, D), BF16)] * 2,
        in_specs=[hbm, vmem, hbm, hbm, hbm, hbm] + [vmem] * 8,
        out_specs=[vmem, vmem],
        scratch_shapes=[
            pltpu.VMEM((NZ, T, D), BF16),
            pltpu.VMEM((NZ, T, 2 * E), BF16),
            pltpu.VMEM((NX, 2, NY, 2, GR, 2 * FH), BF16),
            pltpu.VMEM((NX, 2, NY, 2, DR, D), BF16),
            pltpu.VMEM((NX * 2 * NZ * T, FH), BF16),
            pltpu.VMEM((2 * T, 2 * Q), F32),
            wide,
            pltpu.VMEM((2, 7, T, Q), BF16),
            pltpu.VMEM((2, 7, T, Q), BF16),
            pltpu.VMEM((2, 2, T, Q), BF16),
            pltpu.VMEM((2, 2, T, Q), BF16),
            square, square, square, square, square, square, small, small, wide, wide,
            pltpu.VMEM((HEADS // 2, 2 * T, T), BF16),
            pltpu.VMEM((2, 8, N), F32),
            row, row, row, wide,
            state, state, half, half, half, state,
            state, state, half, half, half, state,
            pltpu.SemaphoreType.DMA((5 + D // FH,)),
            pltpu.SemaphoreType.DMA((COPIES,)),
            pltpu.SemaphoreType.DMA((COPIES,)),
        ],
        compiler_params=pltpu.CompilerParams(
            collective_id=0, has_side_effects=True, vmem_limit_bytes=63 * 2**20
        ),
    )(
        tokens, router.T, gate_up, down, shared_gate_up, shared_down, jnp.swapaxes(routes, 1, 2), lengths,
        jnp.swapaxes(steps, 1, 2), writes, reads, decay_rate.reshape(1, -1), skip_gain.reshape(1, -1), cotangent,
    )
    return pl.pallas_call(
        hand_over,
        out_shape=[jax.ShapeDtypeStruct((1, T, D), BF16)] * 2,
        in_specs=[vmem, vmem],
        out_specs=[vmem, vmem],
    )(out, grad)


def solution(mesh):
    return jax.shard_map(
        on_device,
        mesh=mesh,
        in_specs=(
            P("exp", "ctx", None),
            P(),
            P("exp", "ctx", None),
            P("exp", "ctx", None),
            P(),
            P(),
            P("exp", "ctx", None),
            P("exp", None),
            P("exp", "ctx", None),
            P("exp", "ctx", None),
            P("exp", "ctx", None),
            P(),
            P(),
            P("exp", "ctx", None),
        ),
        out_specs=(P("exp", "ctx", None), P("exp", "ctx", None)),
        check_vma=False,
    )
```

```python
import functools

import jax
import jax.numpy as jnp
from jax import lax
from jax.experimental import pallas as pl
from jax.experimental.pallas import tpu as pltpu
from jax.sharding import PartitionSpec as P

highest = lax.Precision.HIGHEST
MESH = pl.DeviceIdType.MESH
F32 = jnp.float32
BF16 = jnp.bfloat16

T = 128
D = 2560
E = 64
K = 8
FH = 256
NZ, NX, NY = 8, 4, 4
GR = D // 8
DR = FH // 8
HEADS = 40
N = 128
Q = D // 4
NEG = -1e30
SLOT = {4: 0, 3: 1, -3: 2, 2: 3, -2: 4, 1: 5, -1: 6, 0: 7}


def head_columns(first, count):
    h = lax.broadcasted_iota(jnp.int32, (N, count), 0)
    c = lax.broadcasted_iota(jnp.int32, (N, count), 1) + first
    return jnp.where((c >= h * 64) & (c < h * 64 + 64), 1.0, 0.0).astype(BF16)


def spread_heads(a, first, count):
    pick = head_columns(first, count)
    hi = a.astype(BF16)
    lo = (a - hi.astype(F32)).astype(BF16)
    return jnp.dot(hi, pick, preferred_element_type=F32) + jnp.dot(lo, pick, preferred_element_type=F32)


def kernel(
    x_hbm, router_ref, gu_hbm, dn_hbm, sgu_hbm, sdn_hbm, idx_ref, len_ref, raw_ref, b_ref, c_ref,
    rate_ref, skip_ref, cot_ref, out_ref, grad_ref,
    xall, gall, wg, wd, hid, part, shared, rr, rl, sr, sl_,
    cum, cumt, dt, dtt, aff, same, bt, ct, carried, closing, wmat, keeps, kown, ksib, skips, intra,
    lown, lsib, town, tin, sown, sin, lownb, lsibb, townb, tinb, sownb, sinb,
    loc, ss, rs,
):
    ctx = lax.axis_index("ctx")
    exp = lax.axis_index("exp")
    z, x = exp // NX, exp % NX
    y, core = ctx // 2, ctx % 2
    zp = {"exp": (exp + NX) % (NX * NZ)}
    zm = {"exp": (exp + NX * (NZ - 1)) % (NX * NZ)}
    xp = {"exp": z * NX + (x + 1) % NX}
    xm = {"exp": z * NX + (x + NX - 1) % NX}
    yp = {"ctx": (ctx + 2) % 8}
    ym = {"ctx": (ctx + 6) % 8}
    sib = {"ctx": ctx + 1 - 2 * core}
    y1, y2, y3 = (y + 1) % NY, (y + 2) % NY, (y + 3) % NY
    other = 1 - core

    counter = [0]

    def rcopy(src, dst, dev, k):
        return pltpu.make_async_remote_copy(
            src_ref=src, dst_ref=dst, send_sem=ss.at[k], recv_sem=rs.at[k],
            device_id=dev, device_id_type=MESH,
        )

    sent = []

    def send(src, dst, dev):
        k = counter[0]
        counter[0] += 1
        c = rcopy(src, dst, dev, k)
        c.start()
        sent.append(c)
        return k

    def arrived(k, region):
        rcopy(region, region, sib, k).wait_recv()

    barrier = pltpu.get_barrier_semaphore()
    for dev in (zp, zm, xp, xm, yp, ym, sib):
        pl.semaphore_signal(barrier, inc=1, device_id=dev, device_id_type=MESH)

    x_own = xall.at[SLOT[0]]
    lx = pltpu.make_async_copy(x_hbm.at[0], x_own, loc.at[0])
    lx.start()
    SG, SU, SD = 0, D, 2 * D
    shared_copies = [
        pltpu.make_async_copy(sgu_hbm.at[:, pl.ds(0, FH)], hid.at[pl.ds(SG, D)], loc.at[3]),
        pltpu.make_async_copy(sgu_hbm.at[:, pl.ds(FH, FH)], hid.at[pl.ds(SU, D)], loc.at[4]),
    ] + [
        pltpu.make_async_copy(
            sdn_hbm.at[:, pl.ds(i * FH, FH)], hid.at[pl.ds(SD + i * FH, FH)], loc.at[5 + i]
        )
        for i in range(D // FH)
    ]
    for c in shared_copies:
        c.start()
    pl.semaphore_wait(barrier, 7)

    kx = {}
    kx[-1] = send(x_hbm.at[0], xall.at[SLOT[-1]], zp)
    kx[1] = send(x_hbm.at[0], xall.at[SLOT[1]], zm)

    HC = D // 2
    parts = {"g": (gu_hbm, wg, GR, None), "d0": (dn_hbm, wd, DR, pl.ds(0, HC)), "d1": (dn_hbm, wd, DR, pl.ds(HC, HC))}

    def region(name, slot, e, yy, cc, rows=slice(None)):
        w, cols = parts[name][1], parts[name][3]
        return w.at[slot, e, yy, cc, rows] if cols is None else w.at[slot, e, yy, cc, rows, cols]

    def mine(name, e):
        w, cols = parts[name][0], parts[name][3]
        if e is None:
            return w if cols is None else w.at[:, :, cols]
        return w.at[e] if cols is None else w.at[e, :, cols]

    key = {}
    every = slice(None)

    def zeroth(name):
        key[name, "A", 2] = send(mine(name, 0), region(name, 2, 0, y, core), xp)
        key[name, "A", 1] = send(mine(name, 0), region(name, 1, 0, y, core), xm)
        key[name, "B", 3] = send(mine(name, 1), region(name, 0, 1, y, core), yp)
        key[name, "B", 1] = send(mine(name, 1), region(name, 0, 1, y, core), ym)
        own = 1 if name == "g" else None
        key[name, "S"] = send(mine(name, own), region(name, 0, every if own is None else own, y, core), sib)

    def first_ring(name):
        h = parts[name][2] // 2
        lo_, hi_ = pl.ds(0, h), pl.ds(h, h)
        arrived(key[name, "A", 2], region(name, 2, 0, y, core))
        key[name, "hA", 2] = send(region(name, 2, 0, y, core, lo_), region(name, 3, 0, y, core, lo_), xp)
        arrived(key[name, "A", 1], region(name, 1, 0, y, core))
        key[name, "hA", 1] = send(region(name, 1, 0, y, core, hi_), region(name, 3, 0, y, core, hi_), xm)
        b3, b1 = region(name, 0, 1, y3, core), region(name, 0, 1, y1, core)
        arrived(key[name, "B", 3], b3)
        key[name, "hB", 3] = send(region(name, 0, 1, y3, core, lo_), region(name, 0, 1, y3, core, lo_), yp)
        arrived(key[name, "B", 1], b1)
        key[name, "hB", 1] = send(region(name, 0, 1, y1, core, hi_), region(name, 0, 1, y1, core, hi_), ym)
        key[name, "B3S"] = send(b3, b3, sib)
        key[name, "B1S"] = send(b1, b1, sib)

    def second_ring_a(name):
        h = parts[name][2] // 2
        lo_, hi_ = pl.ds(0, h), pl.ds(h, h)
        arrived(key[name, "hA", 2], region(name, 3, 0, y, core, lo_))
        arrived(key[name, "hA", 1], region(name, 3, 0, y, core, hi_))
        a = region(name, every, 0, y, core)
        key[name, "sA", 3] = send(a, a, yp)
        key[name, "sA", 1] = send(a, a, ym)
        s = region(name, pl.ds(1, 3), 0, y, core)
        key[name, "AS"] = send(s, s, sib)

    def second_ring_b(name):
        h = parts[name][2] // 2
        lo_, hi_ = pl.ds(0, h), pl.ds(h, h)
        arrived(key[name, "hB", 3], region(name, 0, 1, y2, core, lo_))
        arrived(key[name, "hB", 1], region(name, 0, 1, y2, core, hi_))
        b = region(name, 0, 1, every, core)
        key[name, "sB", 2] = send(b, region(name, 2, 1, every, core), xp)
        key[name, "sB", 1] = send(b, region(name, 1, 1, every, core), xm)
        s = region(name, 0, 1, y2, core)
        key[name, "B2S"] = send(s, s, sib)

    half_g = (pl.ds(0, GR // 2), pl.ds(GR // 2, GR // 2))

    def slot_out(s):
        a = region("g", s, 0, y, core)
        key["sA", s, 3] = send(a, a, yp)
        key["sA", s, 1] = send(a, a, ym)

    def slot_on(s):
        b3, b1 = region("g", s, 0, y3, core), region("g", s, 0, y1, core)
        arrived(key["sA", s, 3], b3)
        r = region("g", s, 0, y3, core, half_g[0])
        key["lA", s, 3] = send(r, r, yp)
        arrived(key["sA", s, 1], b1)
        r = region("g", s, 0, y1, core, half_g[1])
        key["lA", s, 1] = send(r, r, ym)
        if s == 3:
            for k, r in (("3y", region("g", 3, 0, y, core)), ("3y3", b3), ("3y1", b1)):
                key["sib", k] = send(r, r, sib)

    def slot_last(s):
        arrived(key["lA", s, 3], region("g", s, 0, y2, core, half_g[0]))
        arrived(key["lA", s, 1], region("g", s, 0, y2, core, half_g[1]))
        r = region("g", s, 0, y2 if s == 3 else every, core)
        key["sib", s] = send(r, r, sib)

    def slot_sibling(s):
        arrived(key["sib", s], region("g", s, 0, y2 if s == 3 else every, other))
        if s == 3:
            for k, yy in (("3y", y), ("3y3", y3), ("3y1", y1)):
                arrived(key["sib", k], region("g", 3, 0, yy, other))

    def second_ring_g():
        arrived(key["g", "hA", 2], region("g", 3, 0, y, core, half_g[0]))
        arrived(key["g", "hA", 1], region("g", 3, 0, y, core, half_g[1]))
        slot_out(3)
        arrived(key["g", "hB", 3], region("g", 0, 1, y2, core, half_g[0]))
        arrived(key["g", "hB", 1], region("g", 0, 1, y2, core, half_g[1]))
        b = region("g", 0, 1, every, core)
        key["g", "sB", 2] = send(b, region("g", 2, 1, every, core), xp)
        key["g", "sB", 1] = send(b, region("g", 1, 1, every, core), xm)
        s = region("g", 0, 1, y2, core)
        key["g", "B2S"] = send(s, s, sib)

    def third_g():
        b2, b1 = region("g", 2, 1, every, core), region("g", 1, 1, every, core)
        arrived(key["g", "sB", 2], b2)
        two = pl.ds(0, 2)
        key["g", "lB", 2] = send(region("g", 2, 1, two, core), region("g", 3, 1, two, core), xp)
        arrived(key["g", "sB", 1], b1)
        two = pl.ds(2, 2)
        key["g", "lB", 1] = send(region("g", 1, 1, two, core), region("g", 3, 1, two, core), xm)
        for k, s in (("tB2", b2), ("tB1", b1)):
            key["g", k] = send(s, s, sib)

    def fourth_g():
        for k, two, cc in ((2, pl.ds(0, 2), 0), (1, pl.ds(2, 2), 1)):
            s = region("g", 3, 1, two, core)
            arrived(key["g", "lB", k], s)
            key["g", "fB", k] = send(s, s, sib)

    def sibling_fourth_g():
        for k, two in ((2, pl.ds(0, 2)), (1, pl.ds(2, 2))):
            arrived(key["g", "fB", k], region("g", 3, 1, two, other))

    def third(name):
        b2, b1 = region(name, 2, 1, every, core), region(name, 1, 1, every, core)
        arrived(key[name, "sB", 2], b2)
        two = pl.ds(0, 2)
        key[name, "lB", 2] = send(region(name, 2, 1, two, core), region(name, 3, 1, two, core), xp)
        arrived(key[name, "sB", 1], b1)
        two = pl.ds(2, 2)
        key[name, "lB", 1] = send(region(name, 1, 1, two, core), region(name, 3, 1, two, core), xm)
        a3, a1 = region(name, every, 0, y3, core), region(name, every, 0, y1, core)
        arrived(key[name, "sA", 3], a3)
        s = region(name, pl.ds(0, 2), 0, y3, core)
        key[name, "lA", 3] = send(s, s, yp)
        arrived(key[name, "sA", 1], a1)
        s = region(name, pl.ds(2, 2), 0, y1, core)
        key[name, "lA", 1] = send(s, s, ym)
        for k, s in (("tB2", b2), ("tB1", b1), ("tA3", a3), ("tA1", a1)):
            key[name, k] = send(s, s, sib)

    def fourth(name):
        arrived(key[name, "lA", 3], region(name, pl.ds(0, 2), 0, y2, core))
        arrived(key[name, "lA", 1], region(name, pl.ds(2, 2), 0, y2, core))
        s = region(name, every, 0, y2, core)
        key[name, "fA"] = send(s, s, sib)
        arrived(key[name, "lB", 2], region(name, 3, 1, pl.ds(0, 2), core))
        arrived(key[name, "lB", 1], region(name, 3, 1, pl.ds(2, 2), core))
        s = region(name, 3, 1, every, core)
        key[name, "fB"] = send(s, s, sib)

    def sibling_first(name):
        arrived(key[name, "S"], region(name, 0, 1 if name == "g" else every, y, other))
        arrived(key[name, "B3S"], region(name, 0, 1, y3, other))
        arrived(key[name, "B1S"], region(name, 0, 1, y1, other))
        arrived(key[name, "B2S"], region(name, 0, 1, y2, other))

    def sibling_third(name):
        arrived(key[name, "tB2"], region(name, 2, 1, every, other))
        arrived(key[name, "tB1"], region(name, 1, 1, every, other))

    def sibling_last(name):
        arrived(key[name, "AS"], region(name, pl.ds(1, 3), 0, y, other))
        arrived(key[name, "tA3"], region(name, every, 0, y3, other))
        arrived(key[name, "tA1"], region(name, every, 0, y1, other))
        arrived(key[name, "fA"], region(name, every, 0, y2, other))
        arrived(key[name, "fB"], region(name, 3, 1, every, other))

    for name in ("g", "d0", "d1"):
        zeroth(name)
    lg = pltpu.make_async_copy(gu_hbm, wg.at[0, :, y, core], loc.at[1])
    ld = pltpu.make_async_copy(dn_hbm, wd.at[0, :, y, core], loc.at[2])
    lg.start()
    ld.start()

    lx.wait()
    xo = x_own[...]
    logits = lax.dot_general(
        router_ref[...], xo, (((1,), (1,)), ((), ())), preferred_element_type=F32
    )
    number_of = lax.broadcasted_iota(jnp.int32, (E, T), 0)
    chosen = jnp.zeros((E, T), F32)
    idx = idx_ref[0]
    for j in range(K):
        chosen = chosen + jnp.where(idx[j : j + 1, :] == number_of, 1.0, 0.0)
    sig = chosen * jax.nn.sigmoid(logits)
    gate = sig / jnp.sum(sig, axis=0, keepdims=True)
    hi = gate.astype(BF16).astype(F32)
    gall[SLOT[0]] = jnp.concatenate([hi, gate - hi], axis=0).T.astype(BF16)
    kg = {}
    kg[-1] = send(gall.at[SLOT[0]], gall.at[SLOT[-1]], zp)
    kg[1] = send(gall.at[SLOT[0]], gall.at[SLOT[1]], zm)

    def shared_expert():
        for c in shared_copies:
            c.wait()
        xo = x_own[...]
        sa = jnp.dot(xo, hid[SG : SG + D], preferred_element_type=F32)
        sb = jnp.dot(xo, hid[SU : SU + D], preferred_element_type=F32)
        sh = (jax.nn.silu(sa) * sb).astype(BF16)
        for i in range(D // FH):
            cols = slice(i * FH, (i + 1) * FH)
            shared[:, cols] = xo[:, cols].astype(F32) + jnp.dot(
                sh, hid[SD + i * FH : SD + (i + 1) * FH], preferred_element_type=F32
            )

    def token_step(d):
        for buf, keys in ((xall, kx), (gall, kg)):
            arrived(keys[-d], buf.at[SLOT[-d]])
            arrived(keys[d], buf.at[SLOT[d]])
            if d < 3:
                keys[-d - 1] = send(buf.at[SLOT[-d]], buf.at[SLOT[-d - 1]], zp)
                keys[d + 1] = send(buf.at[SLOT[d]], buf.at[SLOT[d + 1]], zm)
            else:
                lo_, hi_ = pl.ds(0, T // 2), pl.ds(T // 2, T // 2)
                keys["lo"] = send(buf.at[SLOT[-3], lo_], buf.at[SLOT[4], lo_], zp)
                keys["hi"] = send(buf.at[SLOT[3], hi_], buf.at[SLOT[4], hi_], zm)

    row_i = lax.broadcasted_iota(jnp.int32, (T, T), 0)
    col_i = lax.broadcasted_iota(jnp.int32, (T, T), 1)
    second_f = core == 1
    second_b = core == 0

    def decays():
        dtt[...] = jnp.zeros((N, T), F32)
        dtt[0:HEADS, :] = jax.nn.softplus(raw_ref[0])
        steps = dtt[...].T
        dt[...] = steps
        rate = jnp.concatenate([rate_ref[...], jnp.zeros((1, N - HEADS), F32)], axis=1)
        lower = jnp.where(row_i >= col_i, 1.0, 0.0)
        c = jnp.dot(lower, -steps * rate, precision=highest, preferred_element_type=F32)
        cum[...] = c
        cumt[...] = c.T
        b, cc = b_ref[0], c_ref[0]
        bt[...] = b.astype(F32).T.astype(BF16)
        ct[...] = cc.astype(F32).T.astype(BF16)
        lens = jnp.broadcast_to(len_ref[...].astype(F32), (8, 8))
        before = lax.broadcasted_iota(jnp.int32, (8, 8), 1) < lax.broadcasted_iota(jnp.int32, (8, 8), 0)
        starts = jnp.sum(jnp.where(before, lens, 0.0), axis=1, keepdims=True)
        offset = (ctx * T).astype(F32)
        place = lax.broadcasted_iota(jnp.int32, (8, T), 1).astype(F32) + offset

        def number(p):
            return jnp.sum(jnp.where(starts <= p, 1.0, 0.0), axis=0, keepdims=True)

        doc_row = jnp.broadcast_to(number(place), (T, T))
        doc_col = doc_row.T
        ahead = jnp.broadcast_to(number(place[:, 0:1] - 1.0), (T, T))
        final = jnp.broadcast_to(number(place[:, T - 1 : T]), (T, T))
        same[...] = jnp.where(doc_row == doc_col, 1.0, 0.0)
        end = c[T - 1 : T, :]
        carry = jnp.exp(c) * jnp.where(doc_col == ahead, 1.0, 0.0)
        close = jnp.exp(end - c) * jnp.where(doc_col == final, 1.0, 0.0) * dt[...]
        keep = jnp.exp(end) * jnp.where(final[0:1] == ahead[0:1], 1.0, 0.0)
        keeps[0] = jnp.broadcast_to(keep, (8, N))
        key["keep"] = send(keeps.at[0], keeps.at[1], sib)
        skip = jnp.concatenate([skip_ref[...], jnp.zeros((1, N - HEADS), F32)], axis=1)
        for i in range(4):
            cols = slice(i * Q, (i + 1) * Q)
            carried[:, cols] = spread_heads(carry, i * Q, Q)
            closing[:, cols] = spread_heads(close, i * Q, Q)
            skips[:, cols] = spread_heads(jnp.broadcast_to(skip, (8, N)), i * Q, Q)
            kown[:, cols] = spread_heads(keeps[0], i * Q, Q)
        aff[...] = lax.dot_general(cc, b, (((1,), (1,)), ((), ())), preferred_element_type=F32)

    def column(a, h):
        return jnp.sum(jnp.where(col_i == h, a, 0.0), axis=1, keepdims=True)

    def forward_weights():
        causal = (same[...] > 0.5) & (row_i >= col_i)
        a = aff[...]
        c = cum[...]

        def pair(p, _):
            for j in range(2):
                h = 2 * p + j
                gap = column(c, h) - cumt[pl.ds(h, 1), :]
                w = a * jnp.exp(jnp.where(causal, gap, NEG)) * dtt[pl.ds(h, 1), :]
                wmat[p, j * T : (j + 1) * T, :] = w.astype(BF16)
            return 0

        lax.fori_loop(0, HEADS // 2, pair, 0)

    def gradient_states():
        for i in range(4):
            cols = slice(i * Q, (i + 1) * Q)
            v = (carried[:, cols] * cot_ref[0, :, cols].astype(F32)).astype(BF16)
            lownb[:, cols] = jnp.dot(ct[...], v, preferred_element_type=F32).astype(BF16)
        key["lb"] = send(lownb, lsibb, sib)
        arrived(key["keep"], keeps.at[1])
        for i in range(4):
            cols = slice(i * Q, (i + 1) * Q)
            ksib[:, cols] = spread_heads(keeps[1], i * Q, Q)

    rows_own = pl.ds(pl.multiple_of(core * 64, 64), 64)
    rows_other = pl.ds(pl.multiple_of(other * 64, 64), 64)

    def chip_state(cols, lo_, ls, to, second):
        ko, ks = kown[0:1, cols], ksib[0:1, cols]
        one = jnp.ones_like(ko)
        t = jnp.where(second, one, ks) * lo_[rows_own, cols].astype(F32)
        t = t + jnp.where(second, ko, one) * ls[rows_own, cols].astype(F32)
        to[:, cols] = t.astype(BF16)

    def passed_on(cols, to, ti, so):
        k = kown[0:1, cols] * ksib[0:1, cols]
        so[:, cols] = (to[:, cols].astype(F32) + k * ti[:, cols].astype(F32)).astype(BF16)

    def entering(cols, ls, si, second):
        ks = ksib[0:1, cols]
        s = jnp.where(second, ks, jnp.ones_like(ks)) * si[:, cols].astype(F32)
        s = s + jnp.where(second, 1.0, 0.0) * ls[:, cols].astype(F32)
        return s.astype(BF16)

    def gradient_one():
        arrived(key["lb"], lsibb)
        for i in range(4):
            chip_state(slice(i * Q, (i + 1) * Q), lownb, lsibb, townb, second_b)
        key["tb"] = send(townb, tinb, ym)

    def gradient_two():
        arrived(key["tb"], tinb)
        for i in range(4):
            passed_on(slice(i * Q, (i + 1) * Q), townb, tinb, sownb)
        key["sb"] = send(sownb, sinb.at[rows_own], ym)

    def gradient_three():
        arrived(key["sb"], sinb.at[rows_own])
        key["ob"] = send(sinb.at[rows_own], sinb.at[rows_own], sib)

    def gradient_four():
        arrived(key["ob"], sinb.at[rows_other])
        causal = (same[...] > 0.5) & (row_i <= col_i)
        b = b_ref[0]
        a = lax.dot_general(b, c_ref[0], (((1,), (1,)), ((), ())), preferred_element_type=F32)
        c = cum[...]
        d = dt[...]
        left = col_i < 64

        def pair(p, _):
            cols = pl.ds(pl.multiple_of(p * N, N), N)
            seed = cot_ref[0, :, cols]
            halves = []
            for j in range(2):
                h = 2 * p + j
                gap = cumt[pl.ds(h, 1), :] - column(c, h)
                w = a * jnp.exp(jnp.where(causal, gap, NEG)) * column(d, h)
                halves.append(jnp.dot(w.astype(BF16), seed, preferred_element_type=F32))
            g = jnp.where(left, halves[0], halves[1])
            s = entering(cols, lsibb, sinb, second_b)
            g = g + closing[:, cols] * jnp.dot(b, s, preferred_element_type=F32)
            g = g + skips[0:1, cols] * seed.astype(F32)
            grad_ref[0, :, cols] = g.astype(BF16)
            return 0

        lax.fori_loop(0, HEADS // 2, pair, 0)

    def forward_zero(q, u):
        cols = slice(q * Q, (q + 1) * Q)
        v = (closing[:, cols] * u.astype(F32)).astype(BF16)
        lown[:, cols] = jnp.dot(bt[...], v, preferred_element_type=F32).astype(BF16)
        key["l", q] = send(lown.at[:, cols], lsib.at[:, cols], sib)

    def forward_inside(q, u):
        left = col_i < 64
        for i in range(Q // N):
            p = q * (Q // N) + i
            pc = slice(p * N, (p + 1) * N)
            up = u[:, i * N : (i + 1) * N]
            r = jnp.dot(wmat[p], up, preferred_element_type=F32)
            intra[:, pc] = jnp.where(left, r[0:T], r[T:]) + skips[0:1, pc] * up.astype(F32)

    def forward_one(q):
        cols = slice(q * Q, (q + 1) * Q)
        arrived(key["l", q], lsib.at[:, cols])
        chip_state(cols, lown, lsib, town, second_f)
        key["t", q] = send(town.at[:, cols], tin.at[:, cols], yp)

    def forward_two(q):
        cols = slice(q * Q, (q + 1) * Q)
        arrived(key["t", q], tin.at[:, cols])
        passed_on(cols, town, tin, sown)
        key["s", q] = send(sown.at[:, cols], sin.at[rows_own, cols], yp)

    def forward_three(q):
        cols = slice(q * Q, (q + 1) * Q)
        arrived(key["s", q], sin.at[rows_own, cols])
        key["o", q] = send(sin.at[rows_own, cols], sin.at[rows_own, cols], sib)

    def forward_four(q):
        cols = slice(q * Q, (q + 1) * Q)
        arrived(key["o", q], sin.at[rows_other, cols])
        s = entering(cols, lsib, sin, second_f)
        r = intra[:, cols] + carried[:, cols] * jnp.dot(c_ref[0], s, preferred_element_type=F32)
        out_ref[0, :, cols] = r.astype(BF16)

    def hidden_tile(n, m, MT):
        slot, e = n // 2, n % 2
        away = jnp.where(slot == 2, 3, jnp.where(slot == 3, 2, slot))
        expert = 2 * (z * NX + (x + away) % NX) + e
        r = lax.broadcasted_iota(jnp.int32, (2 * E, FH), 0)
        sel = jnp.where((r == expert) | (r == expert + E), 1.0, 0.0).astype(BF16)
        xs = xall[pl.ds(m * (MT // T), MT // T)].reshape(MT, D)
        gs = gall[pl.ds(m * (MT // T), MT // T)].reshape(MT, 2 * E)
        w = wg[slot, e].reshape(D, 2 * FH)
        p = jnp.dot(xs, w, preferred_element_type=F32)
        g = jnp.dot(gs, sel, preferred_element_type=F32)
        h = (jax.nn.silu(p[:, :FH]) * p[:, FH:] * g).astype(BF16)
        hid[pl.ds(pl.multiple_of(n * NZ * T + m * MT, MT), MT), :] = h

    def hidden(experts, tiles, rows=256):
        def one(i, _):
            hidden_tile(experts[0] + experts[1] * (i // tiles[1]), tiles[0] + i % tiles[1], rows)
            return 0

        lax.fori_loop(0, experts[2] * tiles[1], one, 0)

    def partial(first, rows, hf, into):
        h = jnp.concatenate([hid[pl.ds(n * NZ * T + first * T, rows), :] for n in range(8)], axis=1)
        w = wd[:, :, :, :, :, hf * HC : (hf + 1) * HC].reshape(8 * FH, HC)
        acc = jnp.dot(h, w, preferred_element_type=F32)
        if into is part:
            part[0:rows, :] = acc
        else:
            into[:, hf * HC : (hf + 1) * HC] += acc

    kr, kl = {}, {}
    c0, c1 = slice(0, Q), slice(Q, 2 * Q)

    def scatter_start(hf):
        partial(SLOT[4], T, hf, part)
        sr[hf, 0] = part[0:T, c0].astype(BF16)
        kr[hf, 0] = send(sr.at[hf, 0], rr.at[hf, 0], zp)
        sl_[hf, 0] = part[0:T, c1].astype(BF16)
        kl[hf, 0] = send(sl_.at[hf, 0], rl.at[hf, 0], zm)
        partial(SLOT[3], 2 * T, hf, part)
        sr[hf, 1] = part[0:T, c1].astype(BF16)
        kr[hf, 1] = send(sr.at[hf, 1], rr.at[hf, 1], zp)
        sl_[hf, 1] = part[T : 2 * T, c0].astype(BF16)
        kl[hf, 1] = send(sl_.at[hf, 1], rl.at[hf, 1], zm)

    def relay(hf, k):
        cr, cl = (c0, c1) if k % 2 == 0 else (c1, c0)
        arrived(kr[hf, k], rr.at[hf, k])
        rr[hf, k] = (rr[hf, k].astype(F32) + part[0:T, cr]).astype(BF16)
        kr[hf, k + 2] = send(rr.at[hf, k], rr.at[hf, k + 2], zp)
        arrived(kl[hf, k], rl.at[hf, k])
        rl[hf, k] = (rl[hf, k].astype(F32) + part[T : 2 * T, cl]).astype(BF16)
        kl[hf, k + 2] = send(rl.at[hf, k], rl.at[hf, k + 2], zm)

    def mixer_in(hf):
        for k in (5, 6):
            arrived(kr[hf, k], rr.at[hf, k])
            arrived(kl[hf, k], rl.at[hf, k])
        us = []
        for i, (a, b) in enumerate(((6, 5), (5, 6))):
            q = 2 * hf + i
            cols = slice(q * Q, (q + 1) * Q)
            u = shared[:, cols] + rr[hf, a].astype(F32) + rl[hf, b].astype(F32)
            us.append(u.astype(BF16))
            forward_zero(q, us[-1])
        for i, u in enumerate(us):
            forward_inside(2 * hf + i, u)

    lg.wait()
    ld.wait()
    shared_expert()
    decays()
    first_ring("g")
    for slot in range(3):
        slot_out(slot)
    first_ring("d0")
    first_ring("d1")
    token_step(1)
    second_ring_g()
    gradient_states()
    forward_weights()
    sibling_first("g")
    hidden((1, 2, 1), (3, 1))
    slot_on(0)
    slot_on(1)
    token_step(2)
    hidden((1, 2, 1), (2, 1))
    slot_on(2)
    token_step(3)
    slot_on(3)
    third_g()
    second_ring_a("d0")
    second_ring_b("d0")
    slot_last(0)
    sibling_third("g")
    hidden((3, 2, 2), (1, 1), 512)
    slot_last(1)
    slot_sibling(0)
    hidden((0, 1, 1), (1, 1), 512)
    for buf, keys in ((xall, kx), (gall, kg)):
        arrived(keys["lo"], buf.at[SLOT[4], pl.ds(0, T // 2)])
        arrived(keys["hi"], buf.at[SLOT[4], pl.ds(T // 2, T // 2)])
    slot_last(2)
    hidden((1, 2, 2), (0, 1), 512)
    slot_sibling(1)
    hidden((2, 1, 1), (1, 1), 512)
    hidden((5, 1, 1), (0, 1), 512)
    hidden((0, 2, 2), (0, 1), 512)
    slot_last(3)
    fourth_g()
    slot_sibling(2)
    hidden((4, 1, 1), (0, 2), 512)
    third("d0")
    second_ring_a("d1")
    second_ring_b("d1")
    slot_sibling(3)
    hidden((6, 1, 1), (0, 2), 512)
    fourth("d0")
    sibling_fourth_g()
    hidden((7, 1, 1), (0, 2), 512)
    sibling_first("d0")
    sibling_third("d0")
    sibling_last("d0")
    scatter_start(0)
    third("d1")
    relay(0, 0)
    partial(SLOT[2], 2 * T, 0, part)
    fourth("d1")
    relay(0, 1)
    relay(0, 2)
    partial(SLOT[1], 2 * T, 0, part)
    relay(0, 3)
    relay(0, 4)
    sibling_first("d1")
    sibling_third("d1")
    sibling_last("d1")
    scatter_start(1)
    partial(SLOT[0], T, 0, shared)
    mixer_in(0)
    relay(1, 0)
    partial(SLOT[2], 2 * T, 1, part)
    gradient_one()
    forward_one(0)
    forward_one(1)
    relay(1, 1)
    relay(1, 2)
    partial(SLOT[1], 2 * T, 1, part)
    gradient_two()
    forward_two(0)
    forward_two(1)
    relay(1, 3)
    relay(1, 4)
    partial(SLOT[0], T, 1, shared)
    forward_three(0)
    forward_three(1)
    gradient_three()
    gradient_four()
    forward_four(0)
    forward_four(1)
    mixer_in(1)
    for stage in (forward_one, forward_two, forward_three, forward_four):
        stage(2)
        stage(3)
    assert counter[0] == COPIES, counter
    for c in sent:
        c.wait_send()


COPIES = 2 + 2 * 27 + (5 + 6 + 16 + 4 + 3 + 3 + 4 + 2) + 2 + 12 + 28 + 1 + 4 + 16


def hand_over(a_ref, b_ref, out_a, out_b):
    out_a[...] = a_ref[...]
    out_b[...] = b_ref[...]


def on_device(
    tokens, router, gate_up, down, shared_gate_up, shared_down, routes, lengths,
    steps, writes, reads, decay_rate, skip_gain, cotangent,
):
    vmem = pl.BlockSpec(memory_space=pltpu.VMEM)
    hbm = pl.BlockSpec(memory_space=pl.ANY)
    wide = pltpu.VMEM((T, D), F32)
    square = pltpu.VMEM((T, N), F32)
    small = pltpu.VMEM((N, N), BF16)
    state = pltpu.VMEM((N, D), BF16)
    half = pltpu.VMEM((N // 2, D), BF16)
    row = pltpu.VMEM((8, D), F32)
    out, grad = pl.pallas_call(
        kernel,
        out_shape=[jax.ShapeDtypeStruct((1, T, D), BF16)] * 2,
        in_specs=[hbm, vmem, hbm, hbm, hbm, hbm] + [vmem] * 8,
        out_specs=[vmem, vmem],
        scratch_shapes=[
            pltpu.VMEM((NZ, T, D), BF16),
            pltpu.VMEM((NZ, T, 2 * E), BF16),
            pltpu.VMEM((NX, 2, NY, 2, GR, 2 * FH), BF16),
            pltpu.VMEM((NX, 2, NY, 2, DR, D), BF16),
            pltpu.VMEM((NX * 2 * NZ * T, FH), BF16),
            pltpu.VMEM((2 * T, 2 * Q), F32),
            wide,
            pltpu.VMEM((2, 7, T, Q), BF16),
            pltpu.VMEM((2, 7, T, Q), BF16),
            pltpu.VMEM((2, 2, T, Q), BF16),
            pltpu.VMEM((2, 2, T, Q), BF16),
            square, square, square, square, square, square, small, small, wide, wide,
            pltpu.VMEM((HEADS // 2, 2 * T, T), BF16),
            pltpu.VMEM((2, 8, N), F32),
            row, row, row, wide,
            state, state, half, half, half, state,
            state, state, half, half, half, state,
            pltpu.SemaphoreType.DMA((5 + D // FH,)),
            pltpu.SemaphoreType.DMA((COPIES,)),
            pltpu.SemaphoreType.DMA((COPIES,)),
        ],
        compiler_params=pltpu.CompilerParams(
            collective_id=0, has_side_effects=True, vmem_limit_bytes=63 * 2**20
        ),
    )(
        tokens, router.T, gate_up, down, shared_gate_up, shared_down, jnp.swapaxes(routes, 1, 2), lengths,
        jnp.swapaxes(steps, 1, 2), writes, reads, decay_rate.reshape(1, -1), skip_gain.reshape(1, -1), cotangent,
    )
    return pl.pallas_call(
        hand_over,
        out_shape=[jax.ShapeDtypeStruct((1, T, D), BF16)] * 2,
        in_specs=[vmem, vmem],
        out_specs=[vmem, vmem],
    )(out, grad)


def solution(mesh):
    return jax.shard_map(
        on_device,
        mesh=mesh,
        in_specs=(
            P("exp", "ctx", None),
            P(),
            P("exp", "ctx", None),
            P("exp", "ctx", None),
            P(),
            P(),
            P("exp", "ctx", None),
            P("exp", None),
            P("exp", "ctx", None),
            P("exp", "ctx", None),
            P("exp", "ctx", None),
            P(),
            P(),
            P("exp", "ctx", None),
        ),
        out_specs=(P("exp", "ctx", None), P("exp", "ctx", None)),
        check_vma=False,
    )
```
